32 devices in a mesh: groups: 2 (over y), blk: 4 (over z), sub: 2 (over x), rep: 2 (over core).
Axes of the slice: x: 2, y: 2, z: 4, core: 2. Of those that a mesh axis runs over, the one named last changes fastest.
Arguments:
- male_features: bfloat16 [32, 65536], P(None, ('groups', 'blk')), parts along dimension 1, may hold values from -4 to 4
- female_features: bfloat16 [32, 65536], P(None, ('groups', 'blk')), parts along dimension 1, may hold values from -4 to 4
- male_mass: float32 [65536], P(('groups', 'blk')), parts along dimension 0, may hold values from 1 to 30
- female_mass: float32 [65536], P(('groups', 'blk')), parts along dimension 0, may hold values from 1 to 30
- base_interaction: float32 [32, 32], replicated, may hold values from -0.1875 to 0.1875
- reform_interaction: float32 [32, 32], replicated, may hold values from -0.1875 to 0.1875
- female_home: int32 [64], P('groups'), parts along dimension 0, may hold values from 0 to 31, as said below
- pair_female: int32 [256], P(('groups', 'blk', 'sub', 'rep')), parts along dimension 0, may hold values from 0 to 31, as said below
- pair_live: int32 [256], P(('groups', 'blk', 'sub', 'rep')), parts along dimension 0, may hold values from 0 to 1, as said below
Outputs:
- male_root: float32 [65536], P(('groups', 'blk')), parts along dimension 0
- female_root: float32 [65536], P(('groups', 'blk')), parts along dimension 0
The draws below stay inside these ranges and needn't reach their ends.
There are 2 independent parts, one for each index of `groups`. The reference program is written for one: setup_inputs(seed, part) draws one part's arguments, and reference() takes and returns one part's arrays. A program takes and returns all parts, laid end to end along the dimension named above; an argument that names none is the same for every part. Nothing has to cross between parts.
Inputs may be any that keep to these rules, and one draw needn't show every extreme that they name: A permutation: female block i is stored as block female_home[i] of the female arrays. `pair_female`: the 8 slots of one device (slots in order of blk, sub, rep) name each male block of its index of blk once; the 4 slots of one male block name distinct female blocks. Among one device's slots at most 2 name female blocks with the same owner (stored block // 8), and on every device some owner is named 2 times. `pair_live`: every male block has a live slot; at each index of blk one device has all its slots live.
All inputs are finite; a program needn't handle non-finite values.
Results may differ from the reference program's by a relative error of at most 0.0003.
Values may be sent and summed in bfloat16 or wider, within the bound.
A program may use at most 128 MiB of HBM per device.

```python
import math
import jax
import jax.numpy as jnp
from jax import lax

F = 32
TB = 1024
MB_DEV = 8
FB_DEV = 8
ITERS = 2
MATES = 4
MALES = 32768
FEMALES = 32768
PAIRS = 128
N_BLK = 4
N_SUB = 2
N_REP = 2


def market_layout(key):
    owners = N_BLK
    mate_count = N_SUB * N_REP
    home_key, offset_key, spread_key, length_key, order_key, full_key = jax.random.split(key, 6)
    female_home = jax.random.permutation(home_key, FB_DEV * owners).astype(jnp.int32)
    offsets = jax.vmap(lambda sub_key: jax.random.permutation(sub_key, owners))(jax.random.split(offset_key, owners)).astype(jnp.int32)
    block_idx = jnp.arange(owners, dtype=jnp.int32)[:, None, None]
    mate_idx = jnp.arange(mate_count, dtype=jnp.int32)[None, :, None]
    slot_idx = jnp.arange(MB_DEV, dtype=jnp.int32)[None, None, :]
    shifts = offsets[block_idx, slot_idx % owners]
    owner_of = (mate_idx + shifts) % owners
    spread = jax.random.randint(spread_key, (owners, owners, MB_DEV), 0, FB_DEV).astype(jnp.int32)
    within = (mate_idx // owners + spread[block_idx, mate_idx % owners, slot_idx]) % FB_DEV
    stored = owner_of * FB_DEV + within
    lengths = jax.random.randint(length_key, (owners, 1, MB_DEV), 1, mate_count + 1).astype(jnp.int32)
    orders = jax.vmap(lambda sub_key: jax.random.permutation(sub_key, mate_count))(jax.random.split(order_key, owners * MB_DEV)).astype(jnp.int32)
    ranks = orders.reshape(owners, MB_DEV, mate_count).transpose(0, 2, 1)
    full_dev = jax.random.randint(full_key, (owners, 1, 1), 0, mate_count).astype(jnp.int32)
    live = ((ranks < lengths) | (mate_idx == full_dev)).astype(jnp.int32)
    inverse = jnp.argsort(female_home).astype(jnp.int32)
    pair_female = inverse[stored].reshape(-1).astype(jnp.int32)
    return (female_home, pair_female, live.reshape(-1))


def draw_female_home(key, part):
    return market_layout(key)[0]


def draw_pair_female(key, part):
    return market_layout(key)[1]


def draw_pair_live(key, part):
    return market_layout(key)[2]


def level_of(stream_key, extent, cuts, smallest, top_value):
    loudness = 1.0
    for dim, blocks in cuts:
        steps = jax.random.uniform(jax.random.fold_in(jax.random.fold_in(stream_key, 6), dim), (blocks,), jnp.float32, smallest / len(cuts), top_value / len(cuts))
        loudness = loudness * jnp.repeat(jnp.exp(steps), extent[dim] // blocks).reshape((-1,) + (1,) * (len(extent) - 1 - dim))
    return loudness


def centred(stream_key, extent, scale, most, cuts=(), held_as=jnp.bfloat16):
    result = scale * jax.random.normal(stream_key, extent, jnp.float32)
    if cuts:
        result = result * level_of(stream_key, extent, cuts, -0.22, 0.18)
    return jnp.clip(result, -most, most).astype(held_as)


def setup_inputs(seed: int = 0, part: int = 0) -> dict:
    streams_of = jax.random.split(jax.random.key(seed), 10)
    part_splits = jax.random.split(jax.random.fold_in(streams_of[9], part), 10)
    male_features = centred(part_splits[0], (F, MALES), 1.0, 4.0, ((1, 4),))
    female_features = centred(part_splits[1], (F, FEMALES), 1.0, 4.0, ((1, 4),))
    male_mass = jnp.clip(jnp.exp(math.log(30.0) - 3.4011974 * jax.random.uniform(part_splits[2], (MALES,), jnp.float32) ** level_of(part_splits[2], (MALES,), ((0, 4),), -0.2, 0.2)), 1.0, 30.0)
    female_mass = jnp.clip(jnp.exp(math.log(30.0) - 3.4011974 * jax.random.uniform(part_splits[3], (FEMALES,), jnp.float32) ** level_of(part_splits[3], (FEMALES,), ((0, 4),), -0.2, 0.2)), 1.0, 30.0)
    base_interaction = centred(streams_of[4], (F, F), (F * F) ** -0.5, 0.1875, (), jnp.float32)
    reform_interaction = centred(streams_of[5], (F, F), (F * F) ** -0.5, 0.1875, (), jnp.float32)
    female_home = draw_female_home(jax.random.fold_in(jax.random.fold_in(streams_of[9], part), 71), part)
    pair_female = draw_pair_female(jax.random.fold_in(jax.random.fold_in(streams_of[9], part), 71), part)
    pair_live = draw_pair_live(jax.random.fold_in(jax.random.fold_in(streams_of[9], part), 71), part)
    return dict(male_features=male_features, female_features=female_features, male_mass=male_mass, female_mass=female_mass, base_interaction=base_interaction, reform_interaction=reform_interaction, female_home=female_home, pair_female=pair_female, pair_live=pair_live)


rows_per_step = 512

def tile_rows(proj_block, fem_block, row_start, height):
    part_rows = lax.slice_in_dim(proj_block, row_start, row_start + height, axis=1)
    scores = lax.dot_general(part_rows, fem_block.astype(jnp.float32), (((0,), (0,)), ((), ())), precision=lax.Precision.HIGHEST, preferred_element_type=jnp.float32)
    return jnp.exp(0.5 * scores - math.log(fem_block.shape[1])).astype(jnp.bfloat16)

def row_partial(proj_block, fem_block, female_vals):
    span_cols = proj_block.shape[1]
    height = min(span_cols, rows_per_step)
    pieces = []
    for row_start in range(0, span_cols, height):
        kernel = tile_rows(proj_block, fem_block, row_start, height)
        pieces.append(jnp.dot(kernel, female_vals, preferred_element_type=jnp.float32))
    return jnp.concatenate(pieces)

def column_partial(proj_block, fem_block, male_vals):
    span_cols = proj_block.shape[1]
    height = min(span_cols, rows_per_step)
    column_sum = jnp.zeros((fem_block.shape[1],), jnp.float32)
    for row_start in range(0, span_cols, height):
        kernel = tile_rows(proj_block, fem_block, row_start, height)
        column_sum = column_sum + jnp.dot(male_vals[row_start:row_start + height], kernel, preferred_element_type=jnp.float32)
    return column_sum

def solve_pot(totals, masses):
    return 2.0 * masses / (totals + jnp.sqrt(totals * totals + 4.0 * masses))

def reference(male_features, female_features, male_mass, female_mass, base_interaction, reform_interaction, female_home, pair_female, pair_live):
    coupling = base_interaction + reform_interaction
    projected = jnp.dot(coupling.T, male_features.astype(jnp.float32), precision=lax.Precision.HIGHEST, preferred_element_type=jnp.float32)
    proj_blocks = projected.reshape(F, MALES // TB, TB).transpose(1, 0, 2)
    fem_blocks = female_features.reshape(F, FEMALES // TB, TB).transpose(1, 0, 2)
    slot_ids = jnp.arange(PAIRS, dtype=jnp.int32)
    male_of = (slot_ids // (MB_DEV * MATES) * MB_DEV + slot_ids % MB_DEV).astype(jnp.int32)
    store_of = female_home[pair_female].astype(jnp.int32)
    live_mask = pair_live.astype(jnp.float32)
    male_masses = male_mass.reshape(MALES // TB, TB)
    female_masses = female_mass.reshape(FEMALES // TB, TB)
    female_pot = jnp.sqrt(female_masses)
    male_pot = jnp.zeros_like(male_masses)
    for sweep_index in range(ITERS):
        female_vals = female_pot.astype(jnp.bfloat16)

        def row_step(running, slot_item):
            male_id, female_id, weight = slot_item
            partial_rows = row_partial(proj_blocks[male_id], fem_blocks[female_id], female_vals[female_id]) * weight
            return (running.at[male_id].add(partial_rows), None)
        row_total, unused_rows = lax.scan(row_step, jnp.zeros((MALES // TB, TB), jnp.float32), (male_of, store_of, live_mask))
        male_pot = solve_pot(row_total, male_masses)
        male_vals = male_pot.astype(jnp.bfloat16)

        def column_step(running, slot_item):
            male_id, female_id, weight = slot_item
            partial_cols = column_partial(proj_blocks[male_id], fem_blocks[female_id], male_vals[male_id]) * weight
            return (running.at[female_id].add(partial_cols), None)
        col_total, unused_cols = lax.scan(column_step, jnp.zeros((FEMALES // TB, TB), jnp.float32), (male_of, store_of, live_mask))
        female_pot = solve_pot(col_total, female_masses)
    male_root = (male_pot / jnp.sqrt(male_masses)).reshape(MALES)
    female_root = (female_pot / jnp.sqrt(female_masses)).reshape(FEMALES)
    return (male_root, female_root)
```

```python
import functools
import math

import jax
import jax.numpy as jnp
from jax import lax
from jax.experimental import pallas as pl
from jax.experimental.pallas import tpu as pltpu
from jax.sharding import PartitionSpec as P

ITERS = 2
MESH = pl.DeviceIdType.MESH


def solve_pot(totals, masses):
    return 2.0 * masses / (totals + jnp.sqrt(totals * totals + 4.0 * masses))


def sweeps(
    sizes,
    male_ref,
    fem_ref,
    mmass_ref,
    fmass_ref,
    base_ref,
    reform_ref,
    pick_ref,
    live_ref,
    mroot_ref,
    froot_ref,
    kern,
    vals,
    lines,
    rows,
    row_in,
    row_out,
    cols,
    col_out,
    col_in,
    vals_out,
    vals_in,
    last_out,
    last_in,
    row_send,
    row_recv,
    col_send,
    col_recv,
    val_send,
    val_recv,
    last_send,
    last_recv,
):
    owners, n_sub, n_rep = sizes
    mates = n_sub * n_rep
    peers = owners * mates
    slots, block = mmass_ref.shape
    stored_blocks = fmass_ref.shape[0]
    feat = male_ref.shape[0]
    width = col_out.shape[-1]
    chunks = block // width
    group = lax.axis_index("groups")
    my_blk = lax.axis_index("blk")
    my_mate = lax.axis_index("sub") * n_rep + lax.axis_index("rep")
    me = my_blk * mates + my_mate

    def place(peer):
        blk = lax.div(peer, mates)
        mate = lax.rem(peer, mates)
        return (group, blk, lax.div(mate, n_rep), lax.rem(mate, n_rep))

    def mate_place(mate):
        return (group, my_blk, lax.div(mate, n_rep), lax.rem(mate, n_rep))

    def wait_all(ref, sem):
        pltpu.make_async_copy(ref, ref, sem).wait()

    barrier = pltpu.get_barrier_semaphore()

    @pl.loop(1, peers)
    def _(step):
        pl.semaphore_signal(
            barrier, inc=1, device_id=place(lax.rem(me + step, peers)), device_id_type=MESH
        )

    pl.semaphore_wait(barrier, peers - 1)

    def to_peers(src_of, dst, send_sem, recv_sem):
        @pl.loop(1, peers)
        def _(step):
            peer = lax.rem(me + step, peers)
            pltpu.make_async_remote_copy(
                src_ref=src_of(peer),
                dst_ref=dst.at[step],
                send_sem=send_sem,
                recv_sem=recv_sem,
                device_id=place(peer),
                device_id_type=MESH,
            ).start()

    def to_mates(src, dst, send_sem, recv_sem):
        @pl.loop(1, mates)
        def _(step):
            pltpu.make_async_remote_copy(
                src_ref=src,
                dst_ref=dst.at[step],
                send_sem=send_sem,
                recv_sem=recv_sem,
                device_id=mate_place(lax.rem(my_mate + step, mates)),
                device_id_type=MESH,
            ).start()

    def my_chunk(ref):
        start = pl.multiple_of(lax.rem(my_mate, chunks) * width, width)
        return ref[:, pl.ds(start, width)]

    def select_vals(turn):
        for owner in range(owners):
            for chunk in range(chunks):
                index = lax.rem(me - (owner * mates + chunk) + peers, peers)
                vals[
                    owner * stored_blocks : (owner + 1) * stored_blocks,
                    chunk * width : (chunk + 1) * width,
                ] = vals_in[turn, index]
        lines[...] = jnp.dot(
            pick_ref[...].astype(jnp.bfloat16),
            vals[...].astype(jnp.bfloat16),
            preferred_element_type=jnp.float32,
        )

    def line_of(slot):
        return jnp.broadcast_to(lines[pl.ds(slot, 1), :], (16, block)).astype(jnp.bfloat16)

    fmass_mine = my_chunk(fmass_ref)
    first = jnp.sqrt(fmass_mine)
    vals_out[0] = first
    vals_in[0, 0] = first
    to_peers(lambda peer: vals_out.at[0], vals_in.at[0], val_send.at[0], val_recv.at[0])
    wait_all(vals_in.at[0, pl.ds(1, peers - 1)], val_recv.at[0])
    select_vals(0)

    coupling = (base_ref[...] + reform_ref[...]) * (0.5 / math.log(2.0))
    shift = math.log2(block) / 16

    for sweep in range(ITERS):

        @pl.loop(0, slots)
        def _(slot):
            line = line_of(slot)
            if sweep == 0:
                fem = fem_ref[slot]
                men = male_ref[:, pl.ds(pl.multiple_of(slot * block, block), block)]
                projected = lax.dot_general(
                    coupling,
                    men.astype(jnp.float32),
                    (((0,), (0,)), ((), ())),
                    precision=lax.Precision.HIGHEST,
                    preferred_element_type=jnp.float32,
                )
                high = projected.astype(jnp.bfloat16).astype(jnp.float32)
                rest = projected - high
                middle = rest.astype(jnp.bfloat16).astype(jnp.float32)
                left = jnp.concatenate(
                    [high, middle, rest - middle, jnp.full((16, block), -shift, jnp.float32)], axis=0
                )
                left = left.T.astype(jnp.bfloat16)
                right = jnp.concatenate(
                    [fem, fem, fem, jnp.ones((16, block), jnp.bfloat16)], axis=0
                )
                height = block // 4
                for part in range(4):
                    span = slice(part * height, (part + 1) * height)
                    scores = jnp.dot(left[span], right, preferred_element_type=jnp.float32)
                    tile = jnp.exp2(scores).astype(jnp.bfloat16)
                    kern[slot, span, :] = tile
                    total = lax.dot_general(
                        line,
                        tile,
                        (((1,), (1,)), ((), ())),
                        preferred_element_type=jnp.float32,
                    )
                    rows[pl.ds(slot, 1), span] = total[0:1]
            else:
                total = lax.dot_general(
                    line,
                    kern[slot],
                    (((1,), (1,)), ((), ())),
                    preferred_element_type=jnp.float32,
                )
                rows[pl.ds(slot, 1), :] = total[0:1]

        partial = rows[...] * live_ref[...]
        row_out[sweep] = partial
        row_in[sweep, 0] = partial
        to_mates(row_out.at[sweep], row_in.at[sweep], row_send.at[sweep], row_recv.at[sweep])
        wait_all(row_in.at[sweep, pl.ds(1, mates - 1)], row_recv.at[sweep])
        totals = row_in[sweep, lax.rem(my_mate + mates, mates)]
        for mate in range(1, mates):
            totals = totals + row_in[sweep, lax.rem(my_mate - mate + mates, mates)]
        male_pot = solve_pot(totals, mmass_ref[...])
        lines[...] = male_pot
        if sweep == ITERS - 1:
            mroot_ref[...] = male_pot / jnp.sqrt(mmass_ref[...])

        @pl.loop(0, slots)
        def _(slot):
            total = jnp.dot(line_of(slot), kern[slot], preferred_element_type=jnp.float32)
            cols[pl.ds(slot, 1), :] = total[0:1]

        dense = lax.dot_general(
            pick_ref[...] * live_ref[...],
            cols[...],
            (((0,), (0,)), ((), ())),
            precision=lax.Precision.HIGHEST,
            preferred_element_type=jnp.float32,
        )
        for owner in range(owners):
            for mate in range(mates):
                begin = (mate % chunks) * width
                col_out[sweep, owner * mates + mate] = dense[
                    owner * stored_blocks : (owner + 1) * stored_blocks, begin : begin + width
                ]

        col_in[sweep, 0] = col_out[sweep, me]
        to_peers(
            lambda peer: col_out.at[sweep, peer],
            col_in.at[sweep],
            col_send.at[sweep],
            col_recv.at[sweep],
        )
        wait_all(col_in.at[sweep, pl.ds(1, peers - 1)], col_recv.at[sweep])
        col_total = lax.fori_loop(
            1, peers, lambda step, total: total + col_in[sweep, step], col_in[sweep, 0]
        )
        female_pot = solve_pot(col_total, fmass_mine)
        if sweep < ITERS - 1:
            turn = sweep + 1
            vals_out[turn] = female_pot
            vals_in[turn, 0] = female_pot
            to_peers(
                lambda peer: vals_out.at[turn], vals_in.at[turn], val_send.at[turn], val_recv.at[turn]
            )
            wait_all(vals_in.at[turn, pl.ds(1, peers - 1)], val_recv.at[turn])
            select_vals(turn)
        else:
            root = female_pot / jnp.sqrt(fmass_mine)
            last_out[...] = root
            last_in[0] = root
            to_mates(last_out, last_in, last_send, last_recv)
            wait_all(last_in.at[pl.ds(1, mates - 1)], last_recv)
            for chunk in range(chunks):
                froot_ref[:, chunk * width : (chunk + 1) * width] = last_in[
                    lax.rem(my_mate - chunk + mates, mates)
                ]

    for sweep in range(ITERS):
        wait_all(row_in.at[sweep, pl.ds(1, mates - 1)], row_send.at[sweep])
        wait_all(col_in.at[sweep, pl.ds(1, peers - 1)], col_send.at[sweep])
        wait_all(vals_in.at[sweep, pl.ds(1, peers - 1)], val_send.at[sweep])
    wait_all(last_in.at[pl.ds(1, mates - 1)], last_send)


def copy_block(at_ref, from_ref, to_ref):
    to_ref[...] = from_ref[...]


def body(
    male_features,
    female_features,
    male_mass,
    female_mass,
    base_interaction,
    reform_interaction,
    female_home,
    pair_female,
    pair_live,
):
    owners, n_sub, n_rep = (lax.axis_size(name) for name in ("blk", "sub", "rep"))
    mates = n_sub * n_rep
    peers = owners * mates
    slots = pair_female.shape[0]
    block = male_features.shape[1] // slots
    stored_blocks = female_features.shape[1] // block
    width = max(128, block // mates)
    ids = jnp.arange(female_home.shape[0], dtype=jnp.int32)
    stored = jnp.sum(jnp.where(pair_female[:, None] == ids[None, :], female_home[None, :], 0), axis=1)
    pick = (stored[:, None] == ids[None, :]).astype(jnp.float32)
    live = pair_live.astype(jnp.float32)[:, None]
    gathered = lax.all_gather(female_features, "blk")
    wanted = pl.pallas_call(
        copy_block,
        grid_spec=pltpu.PrefetchScalarGridSpec(
            num_scalar_prefetch=1,
            grid=(slots,),
            in_specs=[
                pl.BlockSpec(
                    (1, gathered.shape[1], block),
                    lambda slot, at: (
                        lax.div(at[slot], stored_blocks),
                        0,
                        lax.rem(at[slot], stored_blocks),
                    ),
                )
            ],
            out_specs=pl.BlockSpec((1, gathered.shape[1], block), lambda slot, at: (slot, 0, 0)),
        ),
        out_shape=jax.ShapeDtypeStruct((slots, gathered.shape[1], block), jnp.bfloat16),
        name="wanted_blocks",
    )(stored, gathered)
    vmem = pl.BlockSpec(memory_space=pltpu.VMEM)
    dma = pltpu.SemaphoreType.DMA
    f32 = jnp.float32
    male_root, female_root = pl.pallas_call(
        functools.partial(sweeps, (owners, n_sub, n_rep)),
        out_shape=(
            jax.ShapeDtypeStruct((slots, block), f32),
            jax.ShapeDtypeStruct((stored_blocks, block), f32),
        ),
        in_specs=[vmem] * 8,
        out_specs=(vmem, vmem),
        scratch_shapes=[
            pltpu.VMEM((slots, block, block), jnp.bfloat16),
            pltpu.VMEM((owners * stored_blocks, block), f32),
            pltpu.VMEM((slots, block), f32),
            pltpu.VMEM((slots, block), f32),
            pltpu.VMEM((ITERS, mates, slots, block), f32),
            pltpu.VMEM((ITERS, slots, block), f32),
            pltpu.VMEM((slots, block), f32),
            pltpu.VMEM((ITERS, peers, stored_blocks, width), f32),
            pltpu.VMEM((ITERS, peers, stored_blocks, width), f32),
            pltpu.VMEM((ITERS, stored_blocks, width), f32),
            pltpu.VMEM((ITERS, peers, stored_blocks, width), f32),
            pltpu.VMEM((stored_blocks, width), f32),
            pltpu.VMEM((mates, stored_blocks, width), f32),
            dma((ITERS,)),
            dma((ITERS,)),
            dma((ITERS,)),
            dma((ITERS,)),
            dma((ITERS,)),
            dma((ITERS,)),
            dma,
            dma,
        ],
        compiler_params=pltpu.CompilerParams(
            collective_id=0, has_side_effects=True, vmem_limit_bytes=50 * 2**20
        ),
        name="sweeps",
    )(
        male_features,
        wanted,
        male_mass.reshape(slots, block),
        female_mass.reshape(stored_blocks, block),
        base_interaction,
        reform_interaction,
        pick,
        live,
    )
    return male_root.reshape(-1), female_root.reshape(-1)


def solution(mesh):
    in_specs = (
        P(None, ("groups", "blk")),
        P(None, ("groups", "blk")),
        P(("groups", "blk")),
        P(("groups", "blk")),
        P(),
        P(),
        P("groups"),
        P(("groups", "blk", "sub", "rep")),
        P(("groups", "blk", "sub", "rep")),
    )
    out_specs = (P(("groups", "blk")), P(("groups", "blk")))
    return jax.shard_map(body, mesh=mesh, in_specs=in_specs, out_specs=out_specs, check_vma=False)
```

```python
import functools
import math

import jax
import jax.numpy as jnp
from jax import lax
from jax.experimental import pallas as pl
from jax.experimental.pallas import tpu as pltpu
from jax.sharding import PartitionSpec as P

ITERS = 2
MESH = pl.DeviceIdType.MESH


def solve_pot(totals, masses):
    return 2.0 * masses / (totals + jnp.sqrt(totals * totals + 4.0 * masses))


def sweeps(
    sizes,
    male_ref,
    fem_ref,
    mmass_ref,
    fmass_ref,
    base_ref,
    reform_ref,
    info_ref,
    spot_ref,
    mroot_ref,
    froot_ref,
    kern,
    women,
    men,
    ask_out,
    ask_in,
    fem_out,
    fem_in,
    place,
    pick,
    line_t,
    row_t,
    vals,
    lines,
    place_t,
    row_in,
    row_out,
    cols,
    col_out,
    col_in,
    vals_out,
    vals_in,
    last_out,
    last_in,
    row_send,
    row_recv,
    col_send,
    col_recv,
    val_send,
    val_recv,
    last_send,
    last_recv,
    ask_send,
    ask_recv,
    fem_send,
    fem_recv,
):
    owners, n_sub, n_rep = sizes
    mates = n_sub * n_rep
    peers = owners * mates
    slots, block = mmass_ref.shape
    stored_blocks = fmass_ref.shape[0]
    feat = male_ref.shape[0]
    spots = kern.shape[0]
    depth = spots // owners
    width = col_out.shape[-1]
    chunks = block // width
    group = lax.axis_index("groups")
    my_blk = lax.axis_index("blk")
    my_mate = lax.axis_index("sub") * n_rep + lax.axis_index("rep")
    me = my_blk * mates + my_mate

    def device_of(peer):
        blk = lax.div(peer, mates)
        mate = lax.rem(peer, mates)
        return (group, blk, lax.div(mate, n_rep), lax.rem(mate, n_rep))

    def mate_place(mate):
        return (group, my_blk, lax.div(mate, n_rep), lax.rem(mate, n_rep))

    def wait_all(ref, sem):
        pltpu.make_async_copy(ref, ref, sem).wait()

    barrier = pltpu.get_barrier_semaphore()

    @pl.loop(1, peers)
    def _(step):
        pl.semaphore_signal(
            barrier, inc=1, device_id=device_of(lax.rem(me + step, peers)), device_id_type=MESH
        )

    pl.semaphore_wait(barrier, peers - 1)

    def to_peers(src_of, dst, send_sem, recv_sem):
        @pl.loop(1, peers)
        def _(step):
            peer = lax.rem(me + step, peers)
            pltpu.make_async_remote_copy(
                src_ref=src_of(peer),
                dst_ref=dst.at[step],
                send_sem=send_sem,
                recv_sem=recv_sem,
                device_id=device_of(peer),
                device_id_type=MESH,
            ).start()

    def to_mates(src, dst, send_sem, recv_sem):
        @pl.loop(1, mates)
        def _(step):
            pltpu.make_async_remote_copy(
                src_ref=src,
                dst_ref=dst.at[step],
                send_sem=send_sem,
                recv_sem=recv_sem,
                device_id=mate_place(lax.rem(my_mate + step, mates)),
                device_id_type=MESH,
            ).start()

    def my_chunk(ref):
        start = pl.multiple_of(lax.rem(my_mate, chunks) * width, width)
        return ref[:, pl.ds(start, width)]

    def select_vals(turn):
        for owner in range(owners):
            for chunk in range(chunks):
                index = lax.rem(me - (owner * mates + chunk) + peers, peers)
                vals[
                    owner * stored_blocks : (owner + 1) * stored_blocks,
                    chunk * width : (chunk + 1) * width,
                ] = vals_in[turn, index]
        picked = jnp.dot(
            pick[...].astype(jnp.bfloat16),
            vals[...].astype(jnp.bfloat16),
            preferred_element_type=jnp.float32,
        )
        padded = jnp.concatenate(
            [picked, jnp.zeros((line_t.shape[1] - spots, block), jnp.float32)], axis=0
        )
        line_t[...] = padded.T.astype(jnp.bfloat16)

    def line_of(slot):
        return jnp.broadcast_to(lines[pl.ds(slot, 1), :], (16, block)).astype(jnp.bfloat16)

    fmass_mine = my_chunk(fmass_ref)
    first = jnp.sqrt(fmass_mine)
    vals_out[0] = first
    vals_in[0, 0] = first
    to_peers(lambda peer: vals_out.at[0], vals_in.at[0], val_send.at[0], val_recv.at[0])
    def mix(weights, lines_in):
        total = weights[:, :1] * lines_in[:1, :]
        for index in range(1, lines_in.shape[0]):
            total = total + weights[:, index : index + 1] * lines_in[index : index + 1, :]
        return total

    def equals(line, count):
        lane = lax.broadcasted_iota(jnp.int32, (line.shape[0], count), 1).astype(jnp.float32)
        return jnp.where(line[:, :1] == lane, 1.0, 0.0)

    slot_at, local_at, stored_at, live_at = (spot_ref[index] for index in range(4))
    place[...] = equals(info_ref[0], spots)
    place_t[...] = equals(slot_at, slots)
    pick[...] = equals(stored_at, stored_blocks * owners)
    for step in range(owners):
        ask_out[step, :depth] = local_at[step * depth : (step + 1) * depth]

    @pl.loop(1, owners)
    def _(step):
        to = lax.rem(my_blk - step + owners, owners) * mates + my_mate
        pltpu.make_async_remote_copy(
            src_ref=ask_out.at[step],
            dst_ref=ask_in.at[step],
            send_sem=ask_send,
            recv_sem=ask_recv,
            device_id=device_of(to),
            device_id_type=MESH,
        ).start()

    for index in range(slots):
        men[index * feat : (index + 1) * feat] = male_ref[:, index * block : (index + 1) * block]
    for index in range(stored_blocks):
        women[index * feat : (index + 1) * feat] = fem_ref[:, index * block : (index + 1) * block]

    def choose(line, source):
        total = source.shape[0]
        target = jnp.broadcast_to(line[:, :1], (feat, total)) * feat
        target = target + lax.broadcasted_iota(jnp.int32, (feat, total), 0).astype(jnp.float32)
        column = lax.broadcasted_iota(jnp.int32, (feat, total), 1).astype(jnp.float32)
        hot = jnp.where(column == target, 1.0, 0.0).astype(jnp.bfloat16)
        return jnp.dot(hot, source[...], preferred_element_type=jnp.float32)

    for deep in range(depth):
        fem_in[deep] = choose(ask_out[0, deep : deep + 1], women).astype(jnp.bfloat16)
    wait_all(ask_in.at[pl.ds(1, owners - 1)], ask_recv)

    @pl.loop(1, owners)
    def _(step):
        for deep in range(depth):
            fem_out[step * depth + deep] = choose(
                ask_in[step, deep : deep + 1], women
            ).astype(jnp.bfloat16)
        to = lax.rem(my_blk + step, owners) * mates + my_mate
        pltpu.make_async_remote_copy(
            src_ref=fem_out.at[pl.ds(step * depth, depth)],
            dst_ref=fem_in.at[pl.ds(step * depth, depth)],
            send_sem=fem_send.at[step],
            recv_sem=fem_recv.at[step],
            device_id=device_of(to),
            device_id_type=MESH,
        ).start()

    wait_all(vals_in.at[0, pl.ds(1, peers - 1)], val_recv.at[0])
    select_vals(0)

    coupling = (base_ref[...] + reform_ref[...]) * (0.5 / math.log(2.0))
    shift = math.log2(block) / 16
    column = lax.broadcasted_iota(jnp.int32, (block // 4, line_t.shape[1]), 1)

    for sweep in range(ITERS):

        row_t[...] = jnp.zeros_like(row_t)

        @pl.loop(0, spots)
        def _(spot):
            height = block // 4
            if sweep == 0:

                @pl.when(jnp.logical_and(spot >= depth, lax.rem(spot, depth) == 0))
                def _():
                    step = lax.div(spot, depth)
                    wait_all(fem_in.at[pl.ds(spot, depth)], fem_recv.at[step])

                fem = fem_in[spot]
                projected = lax.dot_general(
                    coupling,
                    choose(spot_ref[0, pl.ds(spot, 1), :], men),
                    (((0,), (0,)), ((), ())),
                    precision=lax.Precision.HIGHEST,
                    preferred_element_type=jnp.float32,
                )
                high = projected.astype(jnp.bfloat16).astype(jnp.float32)
                rest = projected - high
                middle = rest.astype(jnp.bfloat16).astype(jnp.float32)
                left = jnp.concatenate(
                    [high, middle, rest - middle, jnp.full((16, block), -shift, jnp.float32)], axis=0
                )
                left = left.T.astype(jnp.bfloat16)
                right = jnp.concatenate(
                    [fem, fem, fem, jnp.ones((16, block), jnp.bfloat16)], axis=0
                )
            for part in range(4):
                span = slice(part * height, (part + 1) * height)
                if sweep == 0:
                    scores = jnp.dot(left[span], right, preferred_element_type=jnp.float32)
                    tile = jnp.exp2(scores).astype(jnp.bfloat16)
                    kern[spot, span, :] = tile
                else:
                    tile = kern[spot, span, :]
                total = jnp.dot(tile, line_t[...], preferred_element_type=jnp.float32)
                row_t[span, :] = row_t[span, :] + jnp.where(column == spot, total, 0.0)

        partial = mix(place[...], jnp.where(live_at[:, :1] > 0.0, row_t[...].T[:spots], 0.0))
        row_out[sweep] = partial
        row_in[sweep, 0] = partial
        to_mates(row_out.at[sweep], row_in.at[sweep], row_send.at[sweep], row_recv.at[sweep])
        wait_all(row_in.at[sweep, pl.ds(1, mates - 1)], row_recv.at[sweep])
        totals = row_in[sweep, lax.rem(my_mate + mates, mates)]
        for mate in range(1, mates):
            totals = totals + row_in[sweep, lax.rem(my_mate - mate + mates, mates)]
        male_pot = solve_pot(totals, mmass_ref[...])
        lines[...] = mix(place_t[...], male_pot)
        if sweep == ITERS - 1:
            mroot_ref[...] = male_pot / jnp.sqrt(mmass_ref[...])

        @pl.loop(0, spots)
        def _(slot):
            total = jnp.dot(line_of(slot), kern[slot], preferred_element_type=jnp.float32)
            cols[pl.ds(slot, 1), :] = total[0:1]

        dense = lax.dot_general(
            pick[...],
            jnp.where(live_at[:, :1] > 0.0, cols[...], 0.0),
            (((0,), (0,)), ((), ())),
            precision=lax.Precision.HIGHEST,
            preferred_element_type=jnp.float32,
        )
        for owner in range(owners):
            for mate in range(mates):
                begin = (mate % chunks) * width
                col_out[sweep, owner * mates + mate] = dense[
                    owner * stored_blocks : (owner + 1) * stored_blocks, begin : begin + width
                ]

        col_in[sweep, 0] = col_out[sweep, me]
        to_peers(
            lambda peer: col_out.at[sweep, peer],
            col_in.at[sweep],
            col_send.at[sweep],
            col_recv.at[sweep],
        )
        wait_all(col_in.at[sweep, pl.ds(1, peers - 1)], col_recv.at[sweep])
        col_total = lax.fori_loop(
            1, peers, lambda step, total: total + col_in[sweep, step], col_in[sweep, 0]
        )
        female_pot = solve_pot(col_total, fmass_mine)
        if sweep < ITERS - 1:
            turn = sweep + 1
            vals_out[turn] = female_pot
            vals_in[turn, 0] = female_pot
            to_peers(
                lambda peer: vals_out.at[turn], vals_in.at[turn], val_send.at[turn], val_recv.at[turn]
            )
            wait_all(vals_in.at[turn, pl.ds(1, peers - 1)], val_recv.at[turn])
            select_vals(turn)
        else:
            root = female_pot / jnp.sqrt(fmass_mine)
            last_out[...] = root
            last_in[0] = root
            to_mates(last_out, last_in, last_send, last_recv)
            wait_all(last_in.at[pl.ds(1, mates - 1)], last_recv)
            for chunk in range(chunks):
                froot_ref[:, chunk * width : (chunk + 1) * width] = last_in[
                    lax.rem(my_mate - chunk + mates, mates)
                ]

    for sweep in range(ITERS):
        wait_all(row_in.at[sweep, pl.ds(1, mates - 1)], row_send.at[sweep])
        wait_all(col_in.at[sweep, pl.ds(1, peers - 1)], col_send.at[sweep])
        wait_all(vals_in.at[sweep, pl.ds(1, peers - 1)], val_send.at[sweep])
    wait_all(last_in.at[pl.ds(1, mates - 1)], last_send)
    wait_all(ask_in.at[pl.ds(1, owners - 1)], ask_send)

    @pl.loop(1, owners)
    def _(step):
        wait_all(fem_in.at[pl.ds(step * depth, depth)], fem_send.at[step])


def body(
    male_features,
    female_features,
    male_mass,
    female_mass,
    base_interaction,
    reform_interaction,
    female_home,
    pair_female,
    pair_live,
):
    owners, n_sub, n_rep = (lax.axis_size(name) for name in ("blk", "sub", "rep"))
    mates = n_sub * n_rep
    peers = owners * mates
    slots = pair_female.shape[0]
    block = male_features.shape[1] // slots
    stored_blocks = female_features.shape[1] // block
    width = max(128, block // mates)
    ids = jnp.arange(female_home.shape[0], dtype=jnp.int32)
    stored = jnp.sum(jnp.where(pair_female[:, None] == ids[None, :], female_home[None, :], 0), axis=1)
    spot_depth = -(-slots // owners)
    spots = owners * spot_depth
    owner = stored // stored_blocks
    order = jnp.arange(slots, dtype=jnp.int32)
    earlier = (owner[:, None] == owner[None, :]) & (order[None, :] < order[:, None])
    rank = jnp.sum(earlier.astype(jnp.int32), axis=1)
    step = (lax.axis_index("blk") - owner + owners) % owners
    spot = step * spot_depth + rank
    info = jnp.broadcast_to(spot.astype(jnp.float32)[None, :, None], (1, slots, 128))
    at_spot = spot[None, :, None] == jnp.arange(spots, dtype=jnp.int32)[None, None, :]
    facts = jnp.stack([order, stored % stored_blocks, stored, pair_live])
    spot_info = jnp.sum(jnp.where(at_spot, facts[:, :, None], 0), axis=1)
    spot_info = jnp.broadcast_to(spot_info.astype(jnp.float32)[:, :, None], (4, spots, 128))
    feat = male_features.shape[0]
    vmem = pl.BlockSpec(memory_space=pltpu.VMEM)
    dma = pltpu.SemaphoreType.DMA
    f32 = jnp.float32
    male_root, female_root = pl.pallas_call(
        functools.partial(sweeps, (owners, n_sub, n_rep)),
        out_shape=(
            jax.ShapeDtypeStruct((slots, block), f32),
            jax.ShapeDtypeStruct((stored_blocks, block), f32),
        ),
        in_specs=[vmem] * 8,
        out_specs=(vmem, vmem),
        scratch_shapes=[
            pltpu.VMEM((spots, block, block), jnp.bfloat16),
            pltpu.VMEM((stored_blocks * feat, block), jnp.bfloat16),
            pltpu.VMEM((slots * feat, block), jnp.bfloat16),
            pltpu.VMEM((owners, 8, 128), f32),
            pltpu.VMEM((owners, 8, 128), f32),
            pltpu.VMEM((spots, feat, block), jnp.bfloat16),
            pltpu.VMEM((spots, feat, block), jnp.bfloat16),
            pltpu.VMEM((slots, spots), f32),
            pltpu.VMEM((spots, owners * stored_blocks), f32),
            pltpu.VMEM((block, 128), jnp.bfloat16),
            pltpu.VMEM((block, 128), f32),
            pltpu.VMEM((owners * stored_blocks, block), f32),
            pltpu.VMEM((spots, block), f32),
            pltpu.VMEM((spots, slots), f32),
            pltpu.VMEM((ITERS, mates, slots, block), f32),
            pltpu.VMEM((ITERS, slots, block), f32),
            pltpu.VMEM((spots, block), f32),
            pltpu.VMEM((ITERS, peers, stored_blocks, width), f32),
            pltpu.VMEM((ITERS, peers, stored_blocks, width), f32),
            pltpu.VMEM((ITERS, stored_blocks, width), f32),
            pltpu.VMEM((ITERS, peers, stored_blocks, width), f32),
            pltpu.VMEM((stored_blocks, width), f32),
            pltpu.VMEM((mates, stored_blocks, width), f32),
            dma((ITERS,)),
            dma((ITERS,)),
            dma((ITERS,)),
            dma((ITERS,)),
            dma((ITERS,)),
            dma((ITERS,)),
            dma,
            dma,
            dma,
            dma,
            dma((owners,)),
            dma((owners,)),
        ],
        compiler_params=pltpu.CompilerParams(
            collective_id=0, has_side_effects=True, vmem_limit_bytes=50 * 2**20
        ),
        name="sweeps",
    )(
        male_features,
        female_features,
        male_mass.reshape(slots, block),
        female_mass.reshape(stored_blocks, block),
        base_interaction,
        reform_interaction,
        info,
        spot_info,
    )
    return male_root.reshape(-1), female_root.reshape(-1)


def solution(mesh):
    in_specs = (
        P(None, ("groups", "blk")),
        P(None, ("groups", "blk")),
        P(("groups", "blk")),
        P(("groups", "blk")),
        P(),
        P(),
        P("groups"),
        P(("groups", "blk", "sub", "rep")),
        P(("groups", "blk", "sub", "rep")),
    )
    out_specs = (P(("groups", "blk")), P(("groups", "blk")))
    return jax.shard_map(body, mesh=mesh, in_specs=in_specs, out_specs=out_specs, check_vma=False)
```

```python
import functools
import math

import jax
import jax.numpy as jnp
from jax import lax
from jax.experimental import pallas as pl
from jax.experimental.pallas import tpu as pltpu
from jax.sharding import PartitionSpec as P

ITERS = 2
MESH = pl.DeviceIdType.MESH


def solve_pot(totals, masses):
    return 2.0 * masses / (totals + jnp.sqrt(totals * totals + 4.0 * masses))


def sweeps(
    sizes,
    male_ref,
    fem_ref,
    mmass_ref,
    fmass_ref,
    base_ref,
    reform_ref,
    info_ref,
    spot_ref,
    mroot_ref,
    froot_ref,
    kern,
    women,
    men,
    ask_out,
    ask_in,
    fem_out,
    fem_in,
    place,
    pick,
    line_t,
    row_t,
    vals,
    lines,
    place_t,
    row_in,
    row_out,
    cols,
    col_out,
    col_in,
    vals_out,
    vals_in,
    last_out,
    last_in,
    row_send,
    row_recv,
    col_send,
    col_recv,
    val_send,
    val_recv,
    last_send,
    last_recv,
    ask_send,
    ask_recv,
    fem_send,
    fem_recv,
    men_sem,
    women_sem,
):
    owners, n_sub, n_rep = sizes
    mates = n_sub * n_rep
    peers = owners * mates
    slots, block = mmass_ref.shape
    stored_blocks = fmass_ref.shape[0]
    feat = male_ref.shape[0]
    spots = kern.shape[0]
    depth = spots // owners
    width = last_out.shape[-1]
    chunks = block // width
    group = lax.axis_index("groups")
    my_blk = lax.axis_index("blk")
    my_mate = lax.axis_index("sub") * n_rep + lax.axis_index("rep")

    my_sub = lax.axis_index("sub")
    my_rep = lax.axis_index("rep")
    sub_at = [lax.rem(my_sub + shift, n_sub) for shift in range(n_sub)]
    rep_at = [lax.rem(my_rep + shift, n_rep) for shift in range(n_rep)]
    around = [(sub, rep) for sub in range(n_sub) for rep in range(n_rep)]

    def each_blk(act):
        if owners <= 4:
            for step in range(1, owners):
                act(step)
        else:
            pl.loop(1, owners)(act)

    def blk_at(step):
        return lax.rem(my_blk + step, owners)

    def slot_from(blk, mate):
        step = lax.rem(my_blk - blk + owners, owners)
        sub = lax.rem(my_sub - mate // n_rep + n_sub, n_sub)
        return step * mates + sub * n_rep + lax.rem(my_rep - mate % n_rep + n_rep, n_rep)

    def wait_all(ref, sem):
        pltpu.make_async_copy(ref, ref, sem).wait()

    for index in range(slots):
        pltpu.make_async_copy(
            male_ref.at[:, pl.ds(index * block, block)],
            men.at[pl.ds(index * feat, feat)],
            men_sem,
        ).start()
    for index in range(stored_blocks):
        pltpu.make_async_copy(
            fem_ref.at[:, pl.ds(index * block, block)],
            women.at[pl.ds(index * feat, feat)],
            women_sem,
        ).start()

    barrier = pltpu.get_barrier_semaphore()

    def greet(step, skip=False):
        for sub, rep in around[1:] if skip else around:
            pl.semaphore_signal(
                barrier,
                inc=1,
                device_id=(group, blk_at(step), sub_at[sub], rep_at[rep]),
                device_id_type=MESH,
            )

    greet(0, True)
    each_blk(greet)
    pl.semaphore_wait(barrier, peers - 1)

    def to_peers(src_of, dst, send_sem, recv_sem):
        def send(step, skip=False):
            for sub, rep in around[1:] if skip else around:
                pltpu.make_async_remote_copy(
                    src_ref=src_of(step, sub_at[sub] * n_rep + rep_at[rep]),
                    dst_ref=dst.at[step * mates + sub * n_rep + rep],
                    send_sem=send_sem,
                    recv_sem=recv_sem,
                    device_id=(group, blk_at(step), sub_at[sub], rep_at[rep]),
                    device_id_type=MESH,
                ).start()

        each_blk(send)
        send(0, True)

    def to_mates(src, dst, send_sem, recv_sem):
        for sub, rep in around[1:]:
            pltpu.make_async_remote_copy(
                src_ref=src,
                dst_ref=dst.at[sub * n_rep + rep],
                send_sem=send_sem,
                recv_sem=recv_sem,
                device_id=(group, my_blk, sub_at[sub], rep_at[rep]),
                device_id_type=MESH,
            ).start()

    def my_chunk(ref):
        start = pl.multiple_of(lax.rem(my_mate, chunks) * width, width)
        return ref[:, pl.ds(start, width)]

    def pack(piece):
        parts = [piece[:, begin : begin + 128] for begin in range(0, width, 128)]
        if len(parts) == 1:
            parts = parts * 2
        return jnp.concatenate(parts, axis=0).astype(jnp.bfloat16)

    def unpack(packed):
        tall = packed.astype(jnp.float32)
        return jnp.concatenate(
            [
                tall[index * stored_blocks : (index + 1) * stored_blocks]
                for index in range(width // 128)
            ],
            axis=1,
        )

    def select_vals(turn):
        for owner in range(owners):
            for chunk in range(chunks):
                index = slot_from(owner, chunk)
                vals[
                    owner * stored_blocks : (owner + 1) * stored_blocks,
                    chunk * width : (chunk + 1) * width,
                ] = unpack(vals_in[turn, index])
        picked = jnp.dot(
            pick[...].astype(jnp.bfloat16),
            vals[...].astype(jnp.bfloat16),
            preferred_element_type=jnp.float32,
        )
        padded = jnp.concatenate(
            [picked, jnp.zeros((line_t.shape[1] - spots, block), jnp.float32)], axis=0
        )
        line_t[...] = padded.T.astype(jnp.bfloat16)

    def line_of(slot):
        return jnp.broadcast_to(lines[pl.ds(slot, 1), :], (16, block)).astype(jnp.bfloat16)

    fmass_mine = my_chunk(fmass_ref)
    first = pack(jnp.sqrt(fmass_mine))
    vals_out[0] = first
    vals_in[0, 0] = first
    to_peers(lambda step, mate: vals_out.at[0], vals_in.at[0], val_send.at[0], val_recv.at[0])
    def mix(weights, lines_in):
        total = weights[:, :1] * lines_in[:1, :]
        for index in range(1, lines_in.shape[0]):
            total = total + weights[:, index : index + 1] * lines_in[index : index + 1, :]
        return total

    def equals(line, count):
        lane = lax.broadcasted_iota(jnp.int32, (line.shape[0], count), 1).astype(jnp.float32)
        return jnp.where(line[:, :1] == lane, 1.0, 0.0)

    slot_at, local_at, stored_at, live_at = (spot_ref[index] for index in range(4))
    place[...] = equals(info_ref[0], spots)
    place_t[...] = equals(slot_at, slots)
    pick[...] = equals(stored_at, stored_blocks * owners)
    for step in range(owners):
        ask_out[step, :depth] = local_at[step * depth : (step + 1) * depth]

    def ask(step):
        pltpu.make_async_remote_copy(
            src_ref=ask_out.at[step],
            dst_ref=ask_in.at[step],
            send_sem=ask_send,
            recv_sem=ask_recv,
            device_id=(group, blk_at(owners - step), my_sub, my_rep),
            device_id_type=MESH,
        ).start()

    each_blk(ask)
    wait_all(women, women_sem)

    def choose(line, source):
        total = source.shape[0]
        target = jnp.broadcast_to(line[:, :1], (feat, total)) * feat
        target = target + lax.broadcasted_iota(jnp.int32, (feat, total), 0).astype(jnp.float32)
        column = lax.broadcasted_iota(jnp.int32, (feat, total), 1).astype(jnp.float32)
        hot = jnp.where(column == target, 1.0, 0.0).astype(jnp.bfloat16)
        return jnp.dot(hot, source[...], preferred_element_type=jnp.float32)

    for deep in range(depth):
        fem_in[deep] = choose(ask_out[0, deep : deep + 1], women).astype(jnp.bfloat16)
    wait_all(ask_in.at[pl.ds(1, owners - 1)], ask_recv)

    def reply(step):
        for deep in range(depth):
            fem_out[step * depth + deep] = choose(
                ask_in[step, deep : deep + 1], women
            ).astype(jnp.bfloat16)
        pltpu.make_async_remote_copy(
            src_ref=fem_out.at[pl.ds(step * depth, depth)],
            dst_ref=fem_in.at[pl.ds(step * depth, depth)],
            send_sem=fem_send.at[step],
            recv_sem=fem_recv.at[step],
            device_id=(group, blk_at(step), my_sub, my_rep),
            device_id_type=MESH,
        ).start()

    each_blk(reply)
    wait_all(men, men_sem)

    wait_all(vals_in.at[0, pl.ds(1, peers - 1)], val_recv.at[0])
    select_vals(0)

    coupling = (base_ref[...] + reform_ref[...]) * (0.5 / math.log(2.0))
    shift = math.log2(block) / 16
    column = lax.broadcasted_iota(jnp.int32, (block // 4, line_t.shape[1]), 1)

    for sweep in range(ITERS):

        row_t[...] = jnp.zeros_like(row_t)

        @pl.loop(0, spots)
        def _(spot):
            height = block // 4
            if sweep == 0:

                @pl.when(jnp.logical_and(spot >= depth, lax.rem(spot, depth) == 0))
                def _():
                    step = lax.div(spot, depth)
                    wait_all(fem_in.at[pl.ds(spot, depth)], fem_recv.at[step])

                fem = fem_in[spot]
                projected = lax.dot_general(
                    coupling,
                    choose(spot_ref[0, pl.ds(spot, 1), :], men),
                    (((0,), (0,)), ((), ())),
                    precision=lax.Precision.HIGHEST,
                    preferred_element_type=jnp.float32,
                )
                high = projected.astype(jnp.bfloat16).astype(jnp.float32)
                rest = projected - high
                middle = rest.astype(jnp.bfloat16).astype(jnp.float32)
                left = jnp.concatenate(
                    [high, middle, rest - middle, jnp.full((16, block), -shift, jnp.float32)], axis=0
                )
                left = left.T.astype(jnp.bfloat16)
                right = jnp.concatenate(
                    [fem, fem, fem, jnp.ones((16, block), jnp.bfloat16)], axis=0
                )
            for part in range(4):
                span = slice(part * height, (part + 1) * height)
                if sweep == 0:
                    scores = jnp.dot(left[span], right, preferred_element_type=jnp.float32)
                    tile = jnp.exp2(scores).astype(jnp.bfloat16)
                    kern[spot, span, :] = tile
                else:
                    tile = kern[spot, span, :]
                total = jnp.dot(tile, line_t[...], preferred_element_type=jnp.float32)
                row_t[span, :] = row_t[span, :] + jnp.where(column == spot, total, 0.0)

        partial = mix(place[...], jnp.where(live_at[:, :1] > 0.0, row_t[...].T[:spots], 0.0))
        row_out[sweep] = partial
        row_in[sweep, 0] = partial
        to_mates(row_out.at[sweep], row_in.at[sweep], row_send.at[sweep], row_recv.at[sweep])
        wait_all(row_in.at[sweep, pl.ds(1, mates - 1)], row_recv.at[sweep])
        totals = row_in[sweep, slot_from(my_blk, 0)]
        for mate in range(1, mates):
            totals = totals + row_in[sweep, slot_from(my_blk, mate)]
        male_pot = solve_pot(totals, mmass_ref[...])
        lines[...] = mix(place_t[...], male_pot)
        if sweep == ITERS - 1:
            mroot_ref[...] = male_pot / jnp.sqrt(mmass_ref[...])

        @pl.loop(0, spots)
        def _(slot):
            total = jnp.dot(line_of(slot), kern[slot], preferred_element_type=jnp.float32)
            cols[pl.ds(slot, 1), :] = total[0:1]

        columns = jnp.where(live_at[:, :1] > 0.0, cols[...], 0.0)
        for chunk in range(chunks):
            for step in range(owners):
                span = slice(step * depth, (step + 1) * depth)
                col_out[sweep, chunk, step] = jnp.concatenate(
                    [columns[span, chunk * width : (chunk + 1) * width], local_at[span]], axis=1
                )

        col_in[sweep, 0] = col_out[sweep, lax.rem(my_mate, chunks), 0]
        to_peers(
            lambda step, mate: col_out.at[
                sweep, lax.rem(mate, chunks), lax.rem(owners - step, owners)
            ],
            col_in.at[sweep],
            col_send.at[sweep],
            col_recv.at[sweep],
        )
        wait_all(col_in.at[sweep, pl.ds(1, peers - 1)], col_recv.at[sweep])
        blocks_row = lax.broadcasted_iota(jnp.int32, (stored_blocks, 128), 0).astype(jnp.float32)

        def gather_piece(step, total):
            piece = col_in[sweep, step]
            for deep in range(depth):
                here = jnp.where(blocks_row == piece[deep : deep + 1, width:], 1.0, 0.0)
                here = jnp.concatenate([here] * (width // 128), axis=1)
                total = total + here * piece[deep : deep + 1, :width]
            return total

        col_total = lax.fori_loop(
            0, peers, gather_piece, jnp.zeros((stored_blocks, width), jnp.float32)
        )
        female_pot = solve_pot(col_total, fmass_mine)
        if sweep < ITERS - 1:
            turn = sweep + 1
            packed = pack(female_pot)
            vals_out[turn] = packed
            vals_in[turn, 0] = packed
            to_peers(
                lambda step, mate: vals_out.at[turn], vals_in.at[turn], val_send.at[turn], val_recv.at[turn]
            )
            wait_all(vals_in.at[turn, pl.ds(1, peers - 1)], val_recv.at[turn])
            select_vals(turn)
        else:
            root = female_pot / jnp.sqrt(fmass_mine)
            last_out[...] = root
            last_in[0] = root
            to_mates(last_out, last_in, last_send, last_recv)
            wait_all(last_in.at[pl.ds(1, mates - 1)], last_recv)
            for chunk in range(chunks):
                froot_ref[:, chunk * width : (chunk + 1) * width] = last_in[
                    slot_from(my_blk, chunk)
                ]

    for sweep in range(ITERS):
        wait_all(row_in.at[sweep, pl.ds(1, mates - 1)], row_send.at[sweep])
        wait_all(col_in.at[sweep, pl.ds(1, peers - 1)], col_send.at[sweep])
        wait_all(vals_in.at[sweep, pl.ds(1, peers - 1)], val_send.at[sweep])
    wait_all(last_in.at[pl.ds(1, mates - 1)], last_send)
    wait_all(ask_in.at[pl.ds(1, owners - 1)], ask_send)

    @pl.loop(1, owners)
    def _(step):
        wait_all(fem_in.at[pl.ds(step * depth, depth)], fem_send.at[step])


def body(
    male_features,
    female_features,
    male_mass,
    female_mass,
    base_interaction,
    reform_interaction,
    female_home,
    pair_female,
    pair_live,
):
    owners, n_sub, n_rep = (lax.axis_size(name) for name in ("blk", "sub", "rep"))
    mates = n_sub * n_rep
    peers = owners * mates
    slots = pair_female.shape[0]
    block = male_features.shape[1] // slots
    stored_blocks = female_features.shape[1] // block
    width = max(128, block // mates)
    ids = jnp.arange(female_home.shape[0], dtype=jnp.int32)
    stored = jnp.sum(jnp.where(pair_female[:, None] == ids[None, :], female_home[None, :], 0), axis=1)
    spot_depth = -(-slots // owners)
    spots = owners * spot_depth
    owner = stored // stored_blocks
    order = jnp.arange(slots, dtype=jnp.int32)
    earlier = (owner[:, None] == owner[None, :]) & (order[None, :] < order[:, None])
    rank = jnp.sum(earlier.astype(jnp.int32), axis=1)
    step = (lax.axis_index("blk") - owner + owners) % owners
    spot = step * spot_depth + rank
    info = jnp.broadcast_to(spot.astype(jnp.float32)[None, :, None], (1, slots, 128))
    at_spot = spot[None, :, None] == jnp.arange(spots, dtype=jnp.int32)[None, None, :]
    facts = jnp.stack([order, stored % stored_blocks, stored, pair_live])
    spot_info = jnp.sum(jnp.where(at_spot, facts[:, :, None], 0), axis=1)
    spot_info = jnp.broadcast_to(spot_info.astype(jnp.float32)[:, :, None], (4, spots, 128))
    feat = male_features.shape[0]
    vmem = pl.BlockSpec(memory_space=pltpu.VMEM)
    anywhere = pl.BlockSpec(memory_space=pl.ANY)
    dma = pltpu.SemaphoreType.DMA
    f32 = jnp.float32
    male_root, female_root = pl.pallas_call(
        functools.partial(sweeps, (owners, n_sub, n_rep)),
        out_shape=(
            jax.ShapeDtypeStruct((slots, block), f32),
            jax.ShapeDtypeStruct((stored_blocks, block), f32),
        ),
        in_specs=[anywhere] * 2 + [vmem] * 6,
        out_specs=(vmem, vmem),
        scratch_shapes=[
            pltpu.VMEM((spots, block, block), jnp.bfloat16),
            pltpu.VMEM((stored_blocks * feat, block), jnp.bfloat16),
            pltpu.VMEM((slots * feat, block), jnp.bfloat16),
            pltpu.VMEM((owners, 8, 128), f32),
            pltpu.VMEM((owners, 8, 128), f32),
            pltpu.VMEM((spots, feat, block), jnp.bfloat16),
            pltpu.VMEM((spots, feat, block), jnp.bfloat16),
            pltpu.VMEM((slots, spots), f32),
            pltpu.VMEM((spots, owners * stored_blocks), f32),
            pltpu.VMEM((block, 128), jnp.bfloat16),
            pltpu.VMEM((block, 128), f32),
            pltpu.VMEM((owners * stored_blocks, block), f32),
            pltpu.VMEM((spots, block), f32),
            pltpu.VMEM((spots, slots), f32),
            pltpu.VMEM((ITERS, mates, slots, block), f32),
            pltpu.VMEM((ITERS, slots, block), f32),
            pltpu.VMEM((spots, block), f32),
            pltpu.VMEM((ITERS, block // width, owners, spot_depth, width + 128), f32),
            pltpu.VMEM((ITERS, peers, spot_depth, width + 128), f32),
            pltpu.VMEM((ITERS, max(16, stored_blocks * width // 128), 128), jnp.bfloat16),
            pltpu.VMEM((ITERS, peers, max(16, stored_blocks * width // 128), 128), jnp.bfloat16),
            pltpu.VMEM((stored_blocks, width), f32),
            pltpu.VMEM((mates, stored_blocks, width), f32),
            dma((ITERS,)),
            dma((ITERS,)),
            dma((ITERS,)),
            dma((ITERS,)),
            dma((ITERS,)),
            dma((ITERS,)),
            dma,
            dma,
            dma,
            dma,
            dma((owners,)),
            dma((owners,)),
            dma,
            dma,
        ],
        compiler_params=pltpu.CompilerParams(
            collective_id=0, has_side_effects=True, vmem_limit_bytes=50 * 2**20
        ),
        name="sweeps",
    )(
        male_features,
        female_features,
        male_mass.reshape(slots, block),
        female_mass.reshape(stored_blocks, block),
        base_interaction,
        reform_interaction,
        info,
        spot_info,
    )
    return male_root.reshape(-1), female_root.reshape(-1)


def solution(mesh):
    in_specs = (
        P(None, ("groups", "blk")),
        P(None, ("groups", "blk")),
        P(("groups", "blk")),
        P(("groups", "blk")),
        P(),
        P(),
        P("groups"),
        P(("groups", "blk", "sub", "rep")),
        P(("groups", "blk", "sub", "rep")),
    )
    out_specs = (P(("groups", "blk")), P(("groups", "blk")))
    return jax.shard_map(body, mesh=mesh, in_specs=in_specs, out_specs=out_specs, check_vma=False)
```

```python
import functools
import math

import jax
import jax.numpy as jnp
from jax import lax
from jax.experimental import pallas as pl
from jax.experimental.pallas import tpu as pltpu
from jax.sharding import PartitionSpec as P

ITERS = 2
MESH = pl.DeviceIdType.MESH


def solve_pot(totals, masses):
    return 2.0 * masses / (totals + jnp.sqrt(totals * totals + 4.0 * masses))


def sweeps(
    sizes,
    male_ref,
    fem_ref,
    mmass_ref,
    fmass_ref,
    base_ref,
    reform_ref,
    info_ref,
    spot_ref,
    mroot_ref,
    froot_ref,
    kern,
    women,
    men,
    ask_out,
    ask_in,
    fem_out,
    fem_in,
    place,
    pick,
    line_t,
    row_t,
    vals,
    lines,
    place_t,
    row_in,
    row_out,
    cols,
    col_out,
    col_in,
    vals_out,
    vals_in,
    last_out,
    last_in,
    row_send,
    row_recv,
    col_send,
    col_recv,
    val_send,
    val_recv,
    last_send,
    last_recv,
    ask_send,
    ask_recv,
    fem_send,
    fem_recv,
    men_sem,
    women_sem,
):
    owners, n_sub, n_rep = sizes
    mates = n_sub * n_rep
    peers = owners * mates
    slots, block = mmass_ref.shape
    stored_blocks = fmass_ref.shape[0]
    feat = male_ref.shape[0]
    spots = kern.shape[0]
    depth = spots // owners
    width = last_out.shape[-1]
    chunks = block // width
    group = lax.axis_index("groups")
    my_blk = lax.axis_index("blk")
    my_mate = lax.axis_index("sub") * n_rep + lax.axis_index("rep")

    my_sub = lax.axis_index("sub")
    my_rep = lax.axis_index("rep")
    sub_at = [lax.rem(my_sub + shift, n_sub) for shift in range(n_sub)]
    rep_at = [lax.rem(my_rep + shift, n_rep) for shift in range(n_rep)]
    around = [(sub, rep) for sub in range(n_sub) for rep in range(n_rep)]

    def each_blk(act):
        if owners <= 4:
            for step in range(1, owners):
                act(step)
        else:
            pl.loop(1, owners)(act)

    def blk_at(step):
        return lax.rem(my_blk + step, owners)

    def slot_from(blk, mate):
        step = lax.rem(my_blk - blk + owners, owners)
        sub = lax.rem(my_sub - mate // n_rep + n_sub, n_sub)
        return step * mates + sub * n_rep + lax.rem(my_rep - mate % n_rep + n_rep, n_rep)

    def wait_all(ref, sem):
        pltpu.make_async_copy(ref, ref, sem).wait()

    for index in range(slots):
        pltpu.make_async_copy(
            male_ref.at[:, pl.ds(index * block, block)],
            men.at[pl.ds(index * feat, feat)],
            men_sem,
        ).start()
    for index in range(stored_blocks):
        pltpu.make_async_copy(
            fem_ref.at[:, pl.ds(index * block, block)],
            women.at[pl.ds(index * feat, feat)],
            women_sem,
        ).start()

    barrier = pltpu.get_barrier_semaphore()

    def greet(step, skip=False):
        for sub, rep in around[1:] if skip else around:
            pl.semaphore_signal(
                barrier,
                inc=1,
                device_id=(group, blk_at(step), sub_at[sub], rep_at[rep]),
                device_id_type=MESH,
            )

    greet(0, True)
    each_blk(greet)
    pl.semaphore_wait(barrier, peers - 1)

    def to_peers(src_of, dst, send_sem, recv_sem):
        def send(step, skip=False):
            for sub, rep in around[1:] if skip else around:
                pltpu.make_async_remote_copy(
                    src_ref=src_of(step, sub_at[sub] * n_rep + rep_at[rep]),
                    dst_ref=dst.at[step * mates + sub * n_rep + rep],
                    send_sem=send_sem,
                    recv_sem=recv_sem,
                    device_id=(group, blk_at(step), sub_at[sub], rep_at[rep]),
                    device_id_type=MESH,
                ).start()

        each_blk(send)
        send(0, True)

    def to_mates(src, dst, send_sem, recv_sem):
        for sub, rep in around[1:]:
            pltpu.make_async_remote_copy(
                src_ref=src,
                dst_ref=dst.at[sub * n_rep + rep],
                send_sem=send_sem,
                recv_sem=recv_sem,
                device_id=(group, my_blk, sub_at[sub], rep_at[rep]),
                device_id_type=MESH,
            ).start()

    def my_chunk(ref):
        start = pl.multiple_of(lax.rem(my_mate, chunks) * width, width)
        return ref[:, pl.ds(start, width)]

    def pack(piece):
        parts = [piece[:, begin : begin + 128] for begin in range(0, width, 128)]
        if len(parts) == 1:
            parts = parts * 2
        return jnp.concatenate(parts, axis=0).astype(jnp.bfloat16)

    def unpack(packed):
        tall = packed.astype(jnp.float32)
        return jnp.concatenate(
            [
                tall[index * stored_blocks : (index + 1) * stored_blocks]
                for index in range(width // 128)
            ],
            axis=1,
        )

    def select_vals(turn):
        for owner in range(owners):
            for chunk in range(chunks):
                index = slot_from(owner, chunk)
                vals[
                    owner * stored_blocks : (owner + 1) * stored_blocks,
                    chunk * width : (chunk + 1) * width,
                ] = unpack(vals_in[turn, index])
        picked = jnp.dot(
            pick[...].astype(jnp.bfloat16),
            vals[...].astype(jnp.bfloat16),
            preferred_element_type=jnp.float32,
        )
        padded = jnp.concatenate(
            [picked, jnp.zeros((line_t.shape[1] - spots, block), jnp.float32)], axis=0
        )
        line_t[...] = padded.T.astype(jnp.bfloat16)

    middle_row = block // 2
    fmass_mine = my_chunk(fmass_ref)
    first = pack(jnp.sqrt(fmass_mine))
    vals_out[0] = first
    vals_in[0, 0] = first
    to_peers(lambda step, mate: vals_out.at[0], vals_in.at[0], val_send.at[0], val_recv.at[0])
    def mix(weights, lines_in):
        total = weights[:, :1] * lines_in[:1, :]
        for index in range(1, lines_in.shape[0]):
            total = total + weights[:, index : index + 1] * lines_in[index : index + 1, :]
        return total

    def equals(line, count):
        lane = lax.broadcasted_iota(jnp.int32, (line.shape[0], count), 1).astype(jnp.float32)
        return jnp.where(line[:, :1] == lane, 1.0, 0.0)

    slot_at, local_at, stored_at, live_at = (spot_ref[index] for index in range(4))
    place[...] = equals(info_ref[0], spots)
    place_t[...] = equals(slot_at, slots)
    pick[...] = equals(stored_at, stored_blocks * owners)
    for step in range(owners):
        ask_out[step, :depth] = local_at[step * depth : (step + 1) * depth]

    def ask(step):
        pltpu.make_async_remote_copy(
            src_ref=ask_out.at[step],
            dst_ref=ask_in.at[step],
            send_sem=ask_send,
            recv_sem=ask_recv,
            device_id=(group, blk_at(owners - step), my_sub, my_rep),
            device_id_type=MESH,
        ).start()

    each_blk(ask)
    wait_all(women, women_sem)

    def choose(line, source):
        total = source.shape[0]
        target = jnp.broadcast_to(line[:, :1], (feat, total)) * feat
        target = target + lax.broadcasted_iota(jnp.int32, (feat, total), 0).astype(jnp.float32)
        column = lax.broadcasted_iota(jnp.int32, (feat, total), 1).astype(jnp.float32)
        hot = jnp.where(column == target, 1.0, 0.0).astype(jnp.bfloat16)
        return jnp.dot(hot, source[...], preferred_element_type=jnp.float32)

    for deep in range(depth):
        fem_in[deep] = choose(ask_out[0, deep : deep + 1], women).astype(jnp.bfloat16)
    wait_all(ask_in.at[pl.ds(1, owners - 1)], ask_recv)

    def reply(step):
        for deep in range(depth):
            fem_out[step * depth + deep] = choose(
                ask_in[step, deep : deep + 1], women
            ).astype(jnp.bfloat16)
        pltpu.make_async_remote_copy(
            src_ref=fem_out.at[pl.ds(step * depth, depth)],
            dst_ref=fem_in.at[pl.ds(step * depth, depth)],
            send_sem=fem_send.at[step],
            recv_sem=fem_recv.at[step],
            device_id=(group, blk_at(step), my_sub, my_rep),
            device_id_type=MESH,
        ).start()

    each_blk(reply)
    wait_all(men, men_sem)

    wait_all(vals_in.at[0, pl.ds(1, peers - 1)], val_recv.at[0])
    select_vals(0)

    coupling = (base_ref[...] + reform_ref[...]) * (0.5 / math.log(2.0))
    shift = math.log2(block) / 16
    column = lax.broadcasted_iota(jnp.int32, (block // 4, line_t.shape[1]), 1)

    for sweep in range(ITERS):

        row_t[...] = jnp.zeros_like(row_t)
        height = block // 4

        def row_pass(spot, parts):
            if sweep == 0:

                @pl.when(jnp.logical_and(spot >= depth, lax.rem(spot, depth) == 0))
                def _():
                    step = lax.div(spot, depth)
                    wait_all(fem_in.at[pl.ds(spot, depth)], fem_recv.at[step])

                fem = fem_in[spot]
                projected = lax.dot_general(
                    coupling,
                    choose(spot_ref[0, pl.ds(spot, 1), :], men),
                    (((0,), (0,)), ((), ())),
                    precision=lax.Precision.HIGHEST,
                    preferred_element_type=jnp.float32,
                )
                high = projected.astype(jnp.bfloat16).astype(jnp.float32)
                rest = projected - high
                middle = rest.astype(jnp.bfloat16).astype(jnp.float32)
                left = jnp.concatenate(
                    [high, middle, rest - middle, jnp.full((16, block), -shift, jnp.float32)], axis=0
                )
                left = left.T.astype(jnp.bfloat16)
                right = jnp.concatenate(
                    [fem, fem, fem, jnp.ones((16, block), jnp.bfloat16)], axis=0
                )
            for part in parts:
                span = slice(part * height, (part + 1) * height)
                if sweep == 0:
                    scores = jnp.dot(left[span], right, preferred_element_type=jnp.float32)
                    tile = jnp.exp2(scores).astype(jnp.bfloat16)
                    kern[spot, span, :] = tile
                else:
                    tile = kern[spot, span, :]
                total = jnp.dot(tile, line_t[...], preferred_element_type=jnp.float32)
                row_t[span, :] = row_t[span, :] + jnp.where(column == spot, total, 0.0)

        def send_rows(half):
            tall = row_t[half * middle_row : (half + 1) * middle_row, :].T[:spots]
            partial = mix(place[...], jnp.where(live_at[:, :1] > 0.0, tall, 0.0))
            row_out[sweep, half] = partial
            row_in[sweep, half, 0] = partial
            to_mates(
                row_out.at[sweep, half],
                row_in.at[sweep, half],
                row_send.at[sweep, half],
                row_recv.at[sweep, half],
            )

        if sweep == 0:
            pl.loop(0, spots)(lambda spot: row_pass(spot, range(4)))
            send_rows(0)
            send_rows(1)
        else:
            for half in range(2):
                pl.loop(0, spots)(lambda spot: row_pass(spot, range(2 * half, 2 * half + 2)))
                send_rows(half)

        for half in range(2):
            span = slice(half * middle_row, (half + 1) * middle_row)
            wait_all(row_in.at[sweep, half, pl.ds(1, mates - 1)], row_recv.at[sweep, half])
            totals = row_in[sweep, half, slot_from(my_blk, 0)]
            for mate in range(1, mates):
                totals = totals + row_in[sweep, half, slot_from(my_blk, mate)]
            mass = mmass_ref[:, span]
            male_pot = solve_pot(totals, mass)
            lines[:, span] = mix(place_t[...], male_pot)
            if sweep == ITERS - 1:
                mroot_ref[:, span] = male_pot / jnp.sqrt(mass)

            @pl.loop(0, spots)
            def _(spot):
                line = jnp.broadcast_to(lines[pl.ds(spot, 1), span], (16, middle_row))
                total = jnp.dot(
                    line.astype(jnp.bfloat16),
                    kern[spot, span, :],
                    preferred_element_type=jnp.float32,
                )[0:1]
                if half == 0:
                    cols[pl.ds(spot, 1), :] = total
                else:
                    cols[pl.ds(spot, 1), :] = cols[pl.ds(spot, 1), :] + total

        columns = jnp.where(live_at[:, :1] > 0.0, cols[...], 0.0)
        for chunk in range(chunks):
            for step in range(owners):
                span = slice(step * depth, (step + 1) * depth)
                col_out[sweep, chunk, step] = jnp.concatenate(
                    [columns[span, chunk * width : (chunk + 1) * width], local_at[span]], axis=1
                )

        col_in[sweep, 0] = col_out[sweep, lax.rem(my_mate, chunks), 0]
        to_peers(
            lambda step, mate: col_out.at[
                sweep, lax.rem(mate, chunks), lax.rem(owners - step, owners)
            ],
            col_in.at[sweep],
            col_send.at[sweep],
            col_recv.at[sweep],
        )
        wait_all(col_in.at[sweep, pl.ds(1, peers - 1)], col_recv.at[sweep])
        blocks_row = lax.broadcasted_iota(jnp.int32, (stored_blocks, 128), 0).astype(jnp.float32)

        def gather_piece(step, total):
            piece = col_in[sweep, step]
            for deep in range(depth):
                here = jnp.where(blocks_row == piece[deep : deep + 1, width:], 1.0, 0.0)
                here = jnp.concatenate([here] * (width // 128), axis=1)
                total = total + here * piece[deep : deep + 1, :width]
            return total

        col_total = lax.fori_loop(
            0, peers, gather_piece, jnp.zeros((stored_blocks, width), jnp.float32)
        )
        female_pot = solve_pot(col_total, fmass_mine)
        if sweep < ITERS - 1:
            turn = sweep + 1
            packed = pack(female_pot)
            vals_out[turn] = packed
            vals_in[turn, 0] = packed
            to_peers(
                lambda step, mate: vals_out.at[turn], vals_in.at[turn], val_send.at[turn], val_recv.at[turn]
            )
            wait_all(vals_in.at[turn, pl.ds(1, peers - 1)], val_recv.at[turn])
            select_vals(turn)
        else:
            root = female_pot / jnp.sqrt(fmass_mine)
            last_out[...] = root
            last_in[0] = root
            to_mates(last_out, last_in, last_send, last_recv)
            wait_all(last_in.at[pl.ds(1, mates - 1)], last_recv)
            for chunk in range(chunks):
                froot_ref[:, chunk * width : (chunk + 1) * width] = last_in[
                    slot_from(my_blk, chunk)
                ]

    for sweep in range(ITERS):
        for half in range(2):
            wait_all(row_in.at[sweep, half, pl.ds(1, mates - 1)], row_send.at[sweep, half])
        wait_all(col_in.at[sweep, pl.ds(1, peers - 1)], col_send.at[sweep])
        wait_all(vals_in.at[sweep, pl.ds(1, peers - 1)], val_send.at[sweep])
    wait_all(last_in.at[pl.ds(1, mates - 1)], last_send)
    wait_all(ask_in.at[pl.ds(1, owners - 1)], ask_send)

    @pl.loop(1, owners)
    def _(step):
        wait_all(fem_in.at[pl.ds(step * depth, depth)], fem_send.at[step])


def body(
    male_features,
    female_features,
    male_mass,
    female_mass,
    base_interaction,
    reform_interaction,
    female_home,
    pair_female,
    pair_live,
):
    owners, n_sub, n_rep = (lax.axis_size(name) for name in ("blk", "sub", "rep"))
    mates = n_sub * n_rep
    peers = owners * mates
    slots = pair_female.shape[0]
    block = male_features.shape[1] // slots
    stored_blocks = female_features.shape[1] // block
    width = max(128, block // mates)
    ids = jnp.arange(female_home.shape[0], dtype=jnp.int32)
    stored = jnp.sum(jnp.where(pair_female[:, None] == ids[None, :], female_home[None, :], 0), axis=1)
    spot_depth = -(-slots // owners)
    spots = owners * spot_depth
    owner = stored // stored_blocks
    order = jnp.arange(slots, dtype=jnp.int32)
    earlier = (owner[:, None] == owner[None, :]) & (order[None, :] < order[:, None])
    rank = jnp.sum(earlier.astype(jnp.int32), axis=1)
    step = (lax.axis_index("blk") - owner + owners) % owners
    spot = step * spot_depth + rank
    info = jnp.broadcast_to(spot.astype(jnp.float32)[None, :, None], (1, slots, 128))
    at_spot = spot[None, :, None] == jnp.arange(spots, dtype=jnp.int32)[None, None, :]
    facts = jnp.stack([order, stored % stored_blocks, stored, pair_live])
    spot_info = jnp.sum(jnp.where(at_spot, facts[:, :, None], 0), axis=1)
    spot_info = jnp.broadcast_to(spot_info.astype(jnp.float32)[:, :, None], (4, spots, 128))
    feat = male_features.shape[0]
    vmem = pl.BlockSpec(memory_space=pltpu.VMEM)
    anywhere = pl.BlockSpec(memory_space=pl.ANY)
    dma = pltpu.SemaphoreType.DMA
    f32 = jnp.float32
    male_root, female_root = pl.pallas_call(
        functools.partial(sweeps, (owners, n_sub, n_rep)),
        out_shape=(
            jax.ShapeDtypeStruct((slots, block), f32),
            jax.ShapeDtypeStruct((stored_blocks, block), f32),
        ),
        in_specs=[anywhere] * 2 + [vmem] * 6,
        out_specs=(vmem, vmem),
        scratch_shapes=[
            pltpu.VMEM((spots, block, block), jnp.bfloat16),
            pltpu.VMEM((stored_blocks * feat, block), jnp.bfloat16),
            pltpu.VMEM((slots * feat, block), jnp.bfloat16),
            pltpu.VMEM((owners, 8, 128), f32),
            pltpu.VMEM((owners, 8, 128), f32),
            pltpu.VMEM((spots, feat, block), jnp.bfloat16),
            pltpu.VMEM((spots, feat, block), jnp.bfloat16),
            pltpu.VMEM((slots, spots), f32),
            pltpu.VMEM((spots, owners * stored_blocks), f32),
            pltpu.VMEM((block, 128), jnp.bfloat16),
            pltpu.VMEM((block, 128), f32),
            pltpu.VMEM((owners * stored_blocks, block), f32),
            pltpu.VMEM((spots, block), f32),
            pltpu.VMEM((spots, slots), f32),
            pltpu.VMEM((ITERS, 2, mates, slots, block // 2), f32),
            pltpu.VMEM((ITERS, 2, slots, block // 2), f32),
            pltpu.VMEM((spots, block), f32),
            pltpu.VMEM((ITERS, block // width, owners, spot_depth, width + 128), f32),
            pltpu.VMEM((ITERS, peers, spot_depth, width + 128), f32),
            pltpu.VMEM((ITERS, max(16, stored_blocks * width // 128), 128), jnp.bfloat16),
            pltpu.VMEM((ITERS, peers, max(16, stored_blocks * width // 128), 128), jnp.bfloat16),
            pltpu.VMEM((stored_blocks, width), f32),
            pltpu.VMEM((mates, stored_blocks, width), f32),
            dma((ITERS, 2)),
            dma((ITERS, 2)),
            dma((ITERS,)),
            dma((ITERS,)),
            dma((ITERS,)),
            dma((ITERS,)),
            dma,
            dma,
            dma,
            dma,
            dma((owners,)),
            dma((owners,)),
            dma,
            dma,
        ],
        compiler_params=pltpu.CompilerParams(
            collective_id=0, has_side_effects=True, vmem_limit_bytes=60 * 2**20
        ),
        name="sweeps",
    )(
        male_features,
        female_features,
        male_mass.reshape(slots, block),
        female_mass.reshape(stored_blocks, block),
        base_interaction,
        reform_interaction,
        info,
        spot_info,
    )
    return male_root.reshape(-1), female_root.reshape(-1)


def solution(mesh):
    in_specs = (
        P(None, ("groups", "blk")),
        P(None, ("groups", "blk")),
        P(("groups", "blk")),
        P(("groups", "blk")),
        P(),
        P(),
        P("groups"),
        P(("groups", "blk", "sub", "rep")),
        P(("groups", "blk", "sub", "rep")),
    )
    out_specs = (P(("groups", "blk")), P(("groups", "blk")))
    return jax.shard_map(body, mesh=mesh, in_specs=in_specs, out_specs=out_specs, check_vma=False)
```

```python
import functools
import math

import jax
import jax.numpy as jnp
from jax import lax
from jax.experimental import pallas as pl
from jax.experimental.pallas import tpu as pltpu
from jax.sharding import PartitionSpec as P

ITERS = 2
MESH = pl.DeviceIdType.MESH


def solve_pot(totals, masses):
    return 2.0 * masses / (totals + jnp.sqrt(totals * totals + 4.0 * masses))


def sweeps(
    sizes,
    male_ref,
    fem_ref,
    mmass_ref,
    fmass_ref,
    base_ref,
    reform_ref,
    info_ref,
    spot_ref,
    mroot_ref,
    froot_ref,
    kern,
    women,
    men,
    ask_out,
    ask_in,
    fem_out,
    fem_in,
    place,
    pick,
    line_t,
    row_t,
    vals,
    lines,
    place_t,
    row_in,
    row_out,
    cols,
    col_out,
    col_in,
    vals_out,
    vals_in,
    last_out,
    last_in,
    row_send,
    row_recv,
    col_send,
    col_recv,
    val_send,
    val_recv,
    last_send,
    last_recv,
    ask_send,
    ask_recv,
    fem_send,
    fem_recv,
    men_sem,
    women_sem,
):
    owners, n_sub, n_rep = sizes
    mates = n_sub * n_rep
    peers = owners * mates
    slots, block = mmass_ref.shape
    stored_blocks = fmass_ref.shape[0]
    feat = male_ref.shape[0]
    spots = kern.shape[0]
    depth = spots // owners
    width = last_out.shape[-1]
    chunks = block // width
    group = lax.axis_index("groups")
    my_blk = lax.axis_index("blk")
    my_mate = lax.axis_index("sub") * n_rep + lax.axis_index("rep")

    my_sub = lax.axis_index("sub")
    my_rep = lax.axis_index("rep")
    sub_at = [lax.rem(my_sub + shift, n_sub) for shift in range(n_sub)]
    rep_at = [lax.rem(my_rep + shift, n_rep) for shift in range(n_rep)]
    around = [(sub, rep) for sub in range(n_sub) for rep in range(n_rep)]

    def each_blk(act):
        if owners <= 4:
            for step in range(1, owners):
                act(step)
        else:
            pl.loop(1, owners)(act)

    def blk_at(step):
        return lax.rem(my_blk + step, owners)

    def slot_from(blk, mate):
        step = lax.rem(my_blk - blk + owners, owners)
        sub = lax.rem(my_sub - mate // n_rep + n_sub, n_sub)
        return step * mates + sub * n_rep + lax.rem(my_rep - mate % n_rep + n_rep, n_rep)

    def wait_all(ref, sem):
        pltpu.make_async_copy(ref, ref, sem).wait()

    for index in range(slots):
        pltpu.make_async_copy(
            male_ref.at[:, pl.ds(index * block, block)],
            men.at[pl.ds(index * feat, feat)],
            men_sem,
        ).start()
    for index in range(stored_blocks):
        pltpu.make_async_copy(
            fem_ref.at[:, pl.ds(index * block, block)],
            women.at[pl.ds(index * feat, feat)],
            women_sem,
        ).start()

    barrier = pltpu.get_barrier_semaphore()

    def greet(step, skip=False):
        for sub, rep in around[1:] if skip else around:
            pl.semaphore_signal(
                barrier,
                inc=1,
                device_id=(group, blk_at(step), sub_at[sub], rep_at[rep]),
                device_id_type=MESH,
            )

    greet(0, True)
    each_blk(greet)
    pl.semaphore_wait(barrier, peers - 1)

    def to_peers(src_of, dst, send_sem, recv_sem):
        def send(step, skip=False):
            for sub, rep in around[1:] if skip else around:
                pltpu.make_async_remote_copy(
                    src_ref=src_of(step, sub_at[sub] * n_rep + rep_at[rep]),
                    dst_ref=dst.at[step * mates + sub * n_rep + rep],
                    send_sem=send_sem,
                    recv_sem=recv_sem,
                    device_id=(group, blk_at(step), sub_at[sub], rep_at[rep]),
                    device_id_type=MESH,
                ).start()

        each_blk(send)
        send(0, True)

    def to_mates(src, dst, send_sem, recv_sem):
        for sub, rep in around[1:]:
            pltpu.make_async_remote_copy(
                src_ref=src,
                dst_ref=dst.at[sub * n_rep + rep],
                send_sem=send_sem,
                recv_sem=recv_sem,
                device_id=(group, my_blk, sub_at[sub], rep_at[rep]),
                device_id_type=MESH,
            ).start()

    def my_chunk(ref):
        start = pl.multiple_of(lax.rem(my_mate, chunks) * width, width)
        return ref[:, pl.ds(start, width)]

    def pack(piece):
        parts = [piece[:, begin : begin + 128] for begin in range(0, width, 128)]
        if len(parts) == 1:
            parts = parts * 2
        return jnp.concatenate(parts, axis=0).astype(jnp.bfloat16)

    def unpack(packed):
        tall = packed.astype(jnp.float32)
        return jnp.concatenate(
            [
                tall[index * stored_blocks : (index + 1) * stored_blocks]
                for index in range(width // 128)
            ],
            axis=1,
        )

    def select_vals(turn):
        for owner in range(owners):
            for chunk in range(chunks):
                index = slot_from(owner, chunk)
                vals[
                    owner * stored_blocks : (owner + 1) * stored_blocks,
                    chunk * width : (chunk + 1) * width,
                ] = unpack(vals_in[turn, index])
        picked = jnp.dot(
            pick[...].astype(jnp.bfloat16),
            vals[...].astype(jnp.bfloat16),
            preferred_element_type=jnp.float32,
        )
        padded = jnp.concatenate(
            [picked, jnp.zeros((line_t.shape[1] - spots, block), jnp.float32)], axis=0
        )
        line_t[...] = padded.T.astype(jnp.bfloat16)

    def line_of(slot):
        return jnp.broadcast_to(lines[pl.ds(slot, 1), :], (16, block)).astype(jnp.bfloat16)

    fmass_mine = my_chunk(fmass_ref)
    first = pack(jnp.sqrt(fmass_mine))
    vals_out[0] = first
    vals_in[0, 0] = first
    to_peers(lambda step, mate: vals_out.at[0], vals_in.at[0], val_send.at[0], val_recv.at[0])
    def mix(weights, lines_in):
        total = weights[:, :1] * lines_in[:1, :]
        for index in range(1, lines_in.shape[0]):
            total = total + weights[:, index : index + 1] * lines_in[index : index + 1, :]
        return total

    def equals(line, count):
        lane = lax.broadcasted_iota(jnp.int32, (line.shape[0], count), 1).astype(jnp.float32)
        return jnp.where(line[:, :1] == lane, 1.0, 0.0)

    slot_at, local_at, stored_at, live_at = (spot_ref[index] for index in range(4))
    place[...] = equals(info_ref[0], spots)
    place_t[...] = equals(slot_at, slots)
    pick[...] = equals(stored_at, stored_blocks * owners)
    for step in range(owners):
        ask_out[step, :depth] = local_at[step * depth : (step + 1) * depth]

    def ask(step):
        pltpu.make_async_remote_copy(
            src_ref=ask_out.at[step],
            dst_ref=ask_in.at[step],
            send_sem=ask_send,
            recv_sem=ask_recv,
            device_id=(group, blk_at(owners - step), my_sub, my_rep),
            device_id_type=MESH,
        ).start()

    each_blk(ask)
    wait_all(women, women_sem)

    def choose(line, source):
        total = source.shape[0]
        target = jnp.broadcast_to(line[:, :1], (feat, total)) * feat
        target = target + lax.broadcasted_iota(jnp.int32, (feat, total), 0).astype(jnp.float32)
        column = lax.broadcasted_iota(jnp.int32, (feat, total), 1).astype(jnp.float32)
        hot = jnp.where(column == target, 1.0, 0.0).astype(jnp.bfloat16)
        return jnp.dot(hot, source[...], preferred_element_type=jnp.float32)

    for deep in range(depth):
        fem_in[deep] = choose(ask_out[0, deep : deep + 1], women).astype(jnp.bfloat16)
    wait_all(ask_in.at[pl.ds(1, owners - 1)], ask_recv)

    def reply(step):
        for deep in range(depth):
            fem_out[step * depth + deep] = choose(
                ask_in[step, deep : deep + 1], women
            ).astype(jnp.bfloat16)
        pltpu.make_async_remote_copy(
            src_ref=fem_out.at[pl.ds(step * depth, depth)],
            dst_ref=fem_in.at[pl.ds(step * depth, depth)],
            send_sem=fem_send.at[step],
            recv_sem=fem_recv.at[step],
            device_id=(group, blk_at(step), my_sub, my_rep),
            device_id_type=MESH,
        ).start()

    each_blk(reply)
    wait_all(men, men_sem)

    wait_all(vals_in.at[0, pl.ds(1, peers - 1)], val_recv.at[0])
    select_vals(0)

    coupling = (base_ref[...] + reform_ref[...]) * (0.5 / math.log(2.0))
    shift = math.log2(block) / 16
    column = lax.broadcasted_iota(jnp.int32, (block // 4, line_t.shape[1]), 1)

    for sweep in range(ITERS):

        row_t[...] = jnp.zeros_like(row_t)

        @pl.loop(0, spots, unroll=2 if sweep > 0 and spots % 2 == 0 else 1)
        def _(spot):
            height = block // 4
            if sweep == 0:

                @pl.when(jnp.logical_and(spot >= depth, lax.rem(spot, depth) == 0))
                def _():
                    step = lax.div(spot, depth)
                    wait_all(fem_in.at[pl.ds(spot, depth)], fem_recv.at[step])

                fem = fem_in[spot]
                projected = lax.dot_general(
                    coupling,
                    choose(spot_ref[0, pl.ds(spot, 1), :], men),
                    (((0,), (0,)), ((), ())),
                    precision=lax.Precision.HIGHEST,
                    preferred_element_type=jnp.float32,
                )
                high = projected.astype(jnp.bfloat16).astype(jnp.float32)
                rest = projected - high
                middle = rest.astype(jnp.bfloat16).astype(jnp.float32)
                left = jnp.concatenate(
                    [high, middle, rest - middle, jnp.full((16, block), -shift, jnp.float32)], axis=0
                )
                left = left.T.astype(jnp.bfloat16)
                right = jnp.concatenate(
                    [fem, fem, fem, jnp.ones((16, block), jnp.bfloat16)], axis=0
                )
            for part in range(4):
                span = slice(part * height, (part + 1) * height)
                if sweep == 0:
                    scores = jnp.dot(left[span], right, preferred_element_type=jnp.float32)
                    tile = jnp.exp2(scores).astype(jnp.bfloat16)
                    kern[spot, span, :] = tile
                else:
                    tile = kern[spot, span, :]
                total = jnp.dot(tile, line_t[...], preferred_element_type=jnp.float32)
                row_t[span, :] = row_t[span, :] + jnp.where(column == spot, total, 0.0)

        partial = mix(place[...], jnp.where(live_at[:, :1] > 0.0, row_t[...].T[:spots], 0.0))
        row_out[sweep] = partial
        row_in[sweep, 0] = partial
        to_mates(row_out.at[sweep], row_in.at[sweep], row_send.at[sweep], row_recv.at[sweep])
        wait_all(row_in.at[sweep, pl.ds(1, mates - 1)], row_recv.at[sweep])
        totals = row_in[sweep, slot_from(my_blk, 0)]
        for mate in range(1, mates):
            totals = totals + row_in[sweep, slot_from(my_blk, mate)]
        male_pot = solve_pot(totals, mmass_ref[...])
        lines[...] = mix(place_t[...], male_pot)
        if sweep == ITERS - 1:
            mroot_ref[...] = male_pot / jnp.sqrt(mmass_ref[...])

        @pl.loop(0, spots, unroll=2 if spots % 2 == 0 else 1)
        def _(slot):
            total = jnp.dot(line_of(slot), kern[slot], preferred_element_type=jnp.float32)
            cols[pl.ds(slot, 1), :] = total[0:1]

        columns = jnp.where(live_at[:, :1] > 0.0, cols[...], 0.0)
        for chunk in range(chunks):
            for step in range(owners):
                span = slice(step * depth, (step + 1) * depth)
                col_out[sweep, chunk, step] = jnp.concatenate(
                    [columns[span, chunk * width : (chunk + 1) * width], local_at[span]], axis=1
                )

        col_in[sweep, 0] = col_out[sweep, lax.rem(my_mate, chunks), 0]
        to_peers(
            lambda step, mate: col_out.at[
                sweep, lax.rem(mate, chunks), lax.rem(owners - step, owners)
            ],
            col_in.at[sweep],
            col_send.at[sweep],
            col_recv.at[sweep],
        )
        wait_all(col_in.at[sweep, pl.ds(1, peers - 1)], col_recv.at[sweep])
        blocks_row = lax.broadcasted_iota(jnp.int32, (stored_blocks, 128), 0).astype(jnp.float32)

        def gather_piece(step, total):
            piece = col_in[sweep, step]
            for deep in range(depth):
                here = jnp.where(blocks_row == piece[deep : deep + 1, width:], 1.0, 0.0)
                here = jnp.concatenate([here] * (width // 128), axis=1)
                total = total + here * piece[deep : deep + 1, :width]
            return total

        col_total = lax.fori_loop(
            0, peers, gather_piece, jnp.zeros((stored_blocks, width), jnp.float32)
        )
        female_pot = solve_pot(col_total, fmass_mine)
        if sweep < ITERS - 1:
            turn = sweep + 1
            packed = pack(female_pot)
            vals_out[turn] = packed
            vals_in[turn, 0] = packed
            to_peers(
                lambda step, mate: vals_out.at[turn], vals_in.at[turn], val_send.at[turn], val_recv.at[turn]
            )
            wait_all(vals_in.at[turn, pl.ds(1, peers - 1)], val_recv.at[turn])
            select_vals(turn)
        else:
            root = female_pot / jnp.sqrt(fmass_mine)
            last_out[...] = root
            last_in[0] = root
            to_mates(last_out, last_in, last_send, last_recv)
            wait_all(last_in.at[pl.ds(1, mates - 1)], last_recv)
            for chunk in range(chunks):
                froot_ref[:, chunk * width : (chunk + 1) * width] = last_in[
                    slot_from(my_blk, chunk)
                ]

    for sweep in range(ITERS):
        wait_all(row_in.at[sweep, pl.ds(1, mates - 1)], row_send.at[sweep])
        wait_all(col_in.at[sweep, pl.ds(1, peers - 1)], col_send.at[sweep])
        wait_all(vals_in.at[sweep, pl.ds(1, peers - 1)], val_send.at[sweep])
    wait_all(last_in.at[pl.ds(1, mates - 1)], last_send)
    wait_all(ask_in.at[pl.ds(1, owners - 1)], ask_send)

    @pl.loop(1, owners)
    def _(step):
        wait_all(fem_in.at[pl.ds(step * depth, depth)], fem_send.at[step])


def body(
    male_features,
    female_features,
    male_mass,
    female_mass,
    base_interaction,
    reform_interaction,
    female_home,
    pair_female,
    pair_live,
):
    owners, n_sub, n_rep = (lax.axis_size(name) for name in ("blk", "sub", "rep"))
    mates = n_sub * n_rep
    peers = owners * mates
    slots = pair_female.shape[0]
    block = male_features.shape[1] // slots
    stored_blocks = female_features.shape[1] // block
    width = max(128, block // mates)
    ids = jnp.arange(female_home.shape[0], dtype=jnp.int32)
    stored = jnp.sum(jnp.where(pair_female[:, None] == ids[None, :], female_home[None, :], 0), axis=1)
    spot_depth = -(-slots // owners)
    spots = owners * spot_depth
    owner = stored // stored_blocks
    order = jnp.arange(slots, dtype=jnp.int32)
    earlier = (owner[:, None] == owner[None, :]) & (order[None, :] < order[:, None])
    rank = jnp.sum(earlier.astype(jnp.int32), axis=1)
    step = (lax.axis_index("blk") - owner + owners) % owners
    spot = step * spot_depth + rank
    info = jnp.broadcast_to(spot.astype(jnp.float32)[None, :, None], (1, slots, 128))
    at_spot = spot[None, :, None] == jnp.arange(spots, dtype=jnp.int32)[None, None, :]
    facts = jnp.stack([order, stored % stored_blocks, stored, pair_live])
    spot_info = jnp.sum(jnp.where(at_spot, facts[:, :, None], 0), axis=1)
    spot_info = jnp.broadcast_to(spot_info.astype(jnp.float32)[:, :, None], (4, spots, 128))
    feat = male_features.shape[0]
    vmem = pl.BlockSpec(memory_space=pltpu.VMEM)
    anywhere = pl.BlockSpec(memory_space=pl.ANY)
    dma = pltpu.SemaphoreType.DMA
    f32 = jnp.float32
    male_root, female_root = pl.pallas_call(
        functools.partial(sweeps, (owners, n_sub, n_rep)),
        out_shape=(
            jax.ShapeDtypeStruct((slots, block), f32),
            jax.ShapeDtypeStruct((stored_blocks, block), f32),
        ),
        in_specs=[anywhere] * 2 + [vmem] * 6,
        out_specs=(vmem, vmem),
        scratch_shapes=[
            pltpu.VMEM((spots, block, block), jnp.bfloat16),
            pltpu.VMEM((stored_blocks * feat, block), jnp.bfloat16),
            pltpu.VMEM((slots * feat, block), jnp.bfloat16),
            pltpu.VMEM((owners, 8, 128), f32),
            pltpu.VMEM((owners, 8, 128), f32),
            pltpu.VMEM((spots, feat, block), jnp.bfloat16),
            pltpu.VMEM((spots, feat, block), jnp.bfloat16),
            pltpu.VMEM((slots, spots), f32),
            pltpu.VMEM((spots, owners * stored_blocks), f32),
            pltpu.VMEM((block, 128), jnp.bfloat16),
            pltpu.VMEM((block, 128), f32),
            pltpu.VMEM((owners * stored_blocks, block), f32),
            pltpu.VMEM((spots, block), f32),
            pltpu.VMEM((spots, slots), f32),
            pltpu.VMEM((ITERS, mates, slots, block), f32),
            pltpu.VMEM((ITERS, slots, block), f32),
            pltpu.VMEM((spots, block), f32),
            pltpu.VMEM((ITERS, block // width, owners, spot_depth, width + 128), f32),
            pltpu.VMEM((ITERS, peers, spot_depth, width + 128), f32),
            pltpu.VMEM((ITERS, max(16, stored_blocks * width // 128), 128), jnp.bfloat16),
            pltpu.VMEM((ITERS, peers, max(16, stored_blocks * width // 128), 128), jnp.bfloat16),
            pltpu.VMEM((stored_blocks, width), f32),
            pltpu.VMEM((mates, stored_blocks, width), f32),
            dma((ITERS,)),
            dma((ITERS,)),
            dma((ITERS,)),
            dma((ITERS,)),
            dma((ITERS,)),
            dma((ITERS,)),
            dma,
            dma,
            dma,
            dma,
            dma((owners,)),
            dma((owners,)),
            dma,
            dma,
        ],
        compiler_params=pltpu.CompilerParams(
            collective_id=0, has_side_effects=True, vmem_limit_bytes=50 * 2**20
        ),
        name="sweeps",
    )(
        male_features,
        female_features,
        male_mass.reshape(slots, block),
        female_mass.reshape(stored_blocks, block),
        base_interaction,
        reform_interaction,
        info,
        spot_info,
    )
    return male_root.reshape(-1), female_root.reshape(-1)


def solution(mesh):
    in_specs = (
        P(None, ("groups", "blk")),
        P(None, ("groups", "blk")),
        P(("groups", "blk")),
        P(("groups", "blk")),
        P(),
        P(),
        P("groups"),
        P(("groups", "blk", "sub", "rep")),
        P(("groups", "blk", "sub", "rep")),
    )
    out_specs = (P(("groups", "blk")), P(("groups", "blk")))
    return jax.shard_map(body, mesh=mesh, in_specs=in_specs, out_specs=out_specs, check_vma=False)
```
